32 devices in a mesh: shard: 32 (over z, y, x, core).
Axes of the slice: x: 2, y: 2, z: 4, core: 2. Of those that a mesh axis runs over, the one named last changes fastest.
Arguments:
- features: bfloat16 [163840, 400], P('shard'), may hold values from -6 to 6
- counts: int32 [32], P('shard'), may hold values from 1706 to 5120, as said below
- labelled: int32 [163840], P('shard'), may hold values from 0 to 1, as said below
- labels: int32 [163840], P('shard'), may hold values from 0 to 46
- w_branch: float32 [400, 512], P(None, 'shard'), may hold values from -0.625 to 0.625
- w_mid: float32 [2048, 512], P(None, 'shard'), may hold values from -0.125 to 0.125
- w_head: float32 [512, 47], replicated, may hold values from -0.25 to 0.25
- small_params: float32 [9775], replicated, as said below
- mom_branch: float32 [400, 512], P(None, 'shard'), may hold values from -16 to 16
- mom_mid: float32 [2048, 512], P(None, 'shard'), may hold values from -28 to 28
- mom_head: float32 [512, 47], replicated, may hold values from -3072 to 3072
- mom_small: float32 [9775], replicated, may hold values from -20 to 20
- avg_branch: float32 [400, 512], P(None, 'shard'), may hold values from -0.625 to 0.625
- avg_mid: float32 [2048, 512], P(None, 'shard'), may hold values from -0.125 to 0.125
- avg_head: float32 [512, 47], replicated, may hold values from -0.25 to 0.25
- avg_small: float32 [9775], replicated, may hold values from -3 to 3
Outputs:
- logits: float32 [163840, 47], P('shard')
- features_grad: float32 [163840, 400], P('shard')
- grad_branch: float32 [400, 512], P(None, 'shard')
- grad_mid: float32 [2048, 512], P(None, 'shard')
- grad_head: float32 [512, 47], replicated
- grad_small: float32 [9775], replicated
- new_mom_branch: float32 [400, 512], P(None, 'shard')
- new_mom_mid: float32 [2048, 512], P(None, 'shard')
- new_mom_head: float32 [512, 47], replicated
- new_mom_small: float32 [9775], replicated
- new_avg_branch: float32 [400, 512], P(None, 'shard')
- new_avg_mid: float32 [2048, 512], P(None, 'shard')
- new_avg_head: float32 [512, 47], replicated
- new_avg_small: float32 [9775], replicated
- new_branch: float32 [400, 512], P(None, 'shard')
- new_mid: float32 [2048, 512], P(None, 'shard')
- new_head: float32 [512, 47], replicated
- new_small: float32 [9775], replicated
The draws below stay inside these ranges and needn't reach their ends.
Inputs may be any that keep to these rules, and one draw needn't show every extreme that they name: `counts`: filled slots of each device's bucket; some device's bucket is full in every draw. `labelled`: the first slot of every device's bucket is a training node. `small_params`: gains near one, shifts and class bias of both signs, slopes between 0.05 and 0.45.
All inputs are finite; a program needn't handle non-finite values.
Results may differ from the reference program's by a relative error of at most 0.0076.
Values may be sent and summed in bfloat16 or wider, within the bound.
A program may use at most 320 MiB of HBM per device.

```python
import math
import jax
import jax.numpy as jnp
from jax import lax

K = 4
F = 100
H = 512
C = 47
CAP = 5120
NDEV = 32
NODES = 163840
SMALL = 9775


def draw_counts(key, part):
    low_end = CAP // 3
    spread = CAP - low_end - CAP // 16
    device_rank = jnp.arange(NDEV, dtype=jnp.int32)
    base_count = low_end + device_rank * spread // max(NDEV - 1, 1)
    jitter = jax.random.randint(jax.random.fold_in(key, 1), (NDEV,), 0, CAP // 16 + 1)
    filled = jnp.minimum(base_count + jitter, CAP)
    chosen = jax.random.randint(jax.random.fold_in(key, 2), (), 0, NDEV)
    return jnp.where(device_rank == chosen, CAP, filled).astype(jnp.int32)


def draw_labelled(key, part):
    picks = jax.random.randint(jax.random.fold_in(key, 3), (NODES,), 0, 4)
    slot_index = jnp.arange(NODES, dtype=jnp.int32)
    marks = jnp.where(picks < 3, 1, 0)
    return jnp.where(slot_index % CAP == 0, 1, marks).astype(jnp.int32)


def draw_small_params(key, part):
    width = K * H
    gain_one = jax.random.uniform(jax.random.fold_in(key, 4), (width,), jnp.float32, 0.6, 1.4)
    shift_one = 0.3 * jax.random.normal(jax.random.fold_in(key, 5), (width,), jnp.float32)
    slope_one = jax.random.uniform(jax.random.fold_in(key, 6), (width,), jnp.float32, 0.05, 0.45)
    slope_two = jax.random.uniform(jax.random.fold_in(key, 7), (width,), jnp.float32, 0.05, 0.45)
    gain_two = jax.random.uniform(jax.random.fold_in(key, 8), (H,), jnp.float32, 0.6, 1.4)
    shift_two = 0.3 * jax.random.normal(jax.random.fold_in(key, 9), (H,), jnp.float32)
    slope_three = jax.random.uniform(jax.random.fold_in(key, 10), (H,), jnp.float32, 0.05, 0.45)
    class_bias = 0.5 * jax.random.normal(jax.random.fold_in(key, 11), (C,), jnp.float32)
    return jnp.concatenate([gain_one, shift_one, slope_one, slope_two, gain_two, shift_two, slope_three, class_bias])


def touch_ends(values, own_key, low, largest):
    extent = values.shape
    spot = [jax.random.randint(jax.random.fold_in(own_key, axis), (), 0, extent[axis]) for axis in range(len(extent))]
    values = values.at[tuple(spot)].set(low)
    longest = extent.index(max(extent))
    spot[longest] = (spot[longest] + 1) % extent[longest]
    return values.at[tuple(spot)].set(largest)


def block_scale(key, dims, split, least, largest):
    def one(position, blocks):
        heights = jax.random.uniform(jax.random.fold_in(jax.random.fold_in(key, 6), position), (blocks,), jnp.float32, least / len(split), largest / len(split))
        return jnp.repeat(jnp.exp(heights), dims[position] // blocks).reshape((-1,) + (1,) * (len(dims) - position - 1))

    loudness = one(*split[0])
    for cut in split[1:]:
        loudness = loudness * one(*cut)
    return loudness


def centred(stream_key, extent, scale, most, pieces=(), kind=jnp.bfloat16):
    level = block_scale(stream_key, extent, pieces, -0.22, 0.18) if pieces else 1.0
    array = jax.random.normal(stream_key, extent, jnp.float32) * scale * level
    return jnp.minimum(jnp.maximum(array, -most), most).astype(kind)


def setup_inputs(seed: int = 0) -> dict:
    arg_keys = jax.random.split(jax.random.key(seed), 17)
    return {
        "features": centred(arg_keys[0], (NODES, K * F), 1.0, 6.0, ((0, 32),)),
        "counts": draw_counts(jax.random.fold_in(arg_keys[16], 71), 0),
        "labelled": draw_labelled(jax.random.fold_in(arg_keys[16], 71), 0),
        "labels": touch_ends(jax.random.randint(arg_keys[3], (NODES,), 0, C), jax.random.fold_in(arg_keys[3], 1), 0, C - 1).astype(jnp.int32),
        "w_branch": centred(arg_keys[4], (K * F, H), F ** -0.5, 0.625, ((1, 32),), jnp.float32),
        "w_mid": centred(arg_keys[5], (K * H, H), (K * H) ** -0.5, 0.125, ((1, 32),), jnp.float32),
        "w_head": centred(arg_keys[6], (H, C), H ** -0.5, 0.25, (), jnp.float32),
        "small_params": draw_small_params(jax.random.fold_in(arg_keys[16], 71), 0),
        "mom_branch": centred(arg_keys[8], (K * F, H), (0.007 * NODES ** 0.5), 16.0, ((1, 32),), jnp.float32),
        "mom_mid": centred(arg_keys[9], (K * H, H), (0.012 * NODES ** 0.5), 28.0, ((1, 32),), jnp.float32),
        "mom_head": centred(arg_keys[10], (H, C), (0.003 * NODES), 3072.0, (), jnp.float32),
        "mom_small": centred(arg_keys[11], (SMALL,), (0.008 * NODES ** 0.5), 20.0, (), jnp.float32),
        "avg_branch": centred(arg_keys[12], (K * F, H), F ** -0.5, 0.625, ((1, 32),), jnp.float32),
        "avg_mid": centred(arg_keys[13], (K * H, H), (K * H) ** -0.5, 0.125, ((1, 32),), jnp.float32),
        "avg_head": centred(arg_keys[14], (H, C), H ** -0.5, 0.25, (), jnp.float32),
        "avg_small": centred(arg_keys[15], (SMALL,), 0.5, 3.0, (), jnp.float32),
    }


@jax.custom_vjp
def low(v):
    return lax.optimization_barrier(v.astype(jnp.bfloat16)).astype(jnp.float32)

@jax.custom_vjp
def low_back(v):
    return v

def low_keep(v):
    return (low(v), None)

def low_pass(kept, grad):
    return (grad,)

def back_keep(v):
    return (v, None)

def back_low(kept, grad):
    return (low(grad),)
low.defvjp(low_keep, low_pass)
low_back.defvjp(back_keep, back_low)
EPS = 1e-05
MOMENTUM = 0.9
DECAY = 0.9
HIGH = lax.Precision.HIGHEST

def prelu_apply(values_in, slopes):
    return slopes * values_in + (1.0 - slopes) * jax.nn.softplus(values_in)

def split_small(packed):
    width = K * H
    return (packed[:width], packed[width:2 * width], packed[2 * width:3 * width], packed[3 * width:4 * width], packed[4 * width:4 * width + H], packed[4 * width + H:4 * width + 2 * H], packed[4 * width + 2 * H:4 * width + 3 * H], packed[4 * width + 3 * H:])

def nesterov(weight, gradient, momentum_old, average_old, step_rate):
    momentum_new = MOMENTUM * momentum_old + gradient
    weight_new = weight - step_rate * (gradient + MOMENTUM * momentum_new)
    average_new = DECAY * average_old + (1.0 - DECAY) * weight_new
    return (momentum_new, average_new, weight_new)

def reference(features, counts, labelled, labels, w_branch, w_mid, w_head, small_params, mom_branch, mom_mid, mom_head, mom_small, avg_branch, avg_mid, avg_head, avg_small):
    slot_index = jnp.arange(CAP, dtype=jnp.int32)
    bucket = (slot_index[None, :] < counts[:, None]).astype(jnp.float32)
    trained = bucket * labelled.reshape(NDEV, CAP).astype(jnp.float32)
    label_rows = labels.reshape(NDEV, CAP)
    count_fill = jnp.sum(bucket)
    features32 = features.astype(jnp.float32)
    class_ids = jnp.arange(C, dtype=jnp.int32)

    def forward(feats_in, branch_w, mid_w, head_w, packed):
        gain1, shift1, slope1, slope2, gain2, shift2, slope3, head_bias = split_small(packed)
        branch_low = low(branch_w).reshape(K, F, H)
        mid_low = low(mid_w)
        head_low = low(head_w)
        blocks = feats_in.reshape(NDEV, CAP, K, F)

        def gram_block(carry, item):
            block_x, block_b = item
            masked = block_x * block_b[:, None, None]
            totals = carry[0] + lax.optimization_barrier(jnp.sum(masked, axis=0))
            grams = carry[1] + jnp.einsum('nkf,nkg->kfg', masked, block_x, precision=HIGH)
            return ((totals, grams), None)
        start = (jnp.zeros((K, F), feats_in.dtype), jnp.zeros((K, F, F), feats_in.dtype))
        (totals, grams), _ = lax.scan(jax.checkpoint(gram_block), start, (blocks, bucket))
        mean1 = jnp.einsum('kf,kfh->kh', totals, branch_low, precision=HIGH) / count_fill
        second = jnp.einsum('kfh,kfg,kgh->kh', branch_low, grams, branch_low, precision=HIGH) / count_fill
        inv1 = lax.rsqrt(second - mean1 * mean1 + EPS).reshape(K * H)
        mean1 = mean1.reshape(K * H)

        def mid_block(block_x):
            branch_pre = low_back(jnp.einsum('nkf,kfh->nkh', block_x, branch_low, precision=HIGH).reshape(CAP, K * H))
            branch_norm = gain1 * (branch_pre - mean1) * inv1 + shift1
            concat = prelu_apply(prelu_apply(branch_norm, slope1), slope2)
            return low_back(jnp.dot(low(concat), mid_low, precision=HIGH))
        mid_pre = lax.map(jax.checkpoint(mid_block), blocks)
        mean2 = lax.optimization_barrier(jnp.sum(mid_pre * bucket[:, :, None], axis=(0, 1))) / count_fill
        var2 = lax.optimization_barrier(jnp.sum((mid_pre - mean2) ** 2 * bucket[:, :, None], axis=(0, 1))) / count_fill
        inv2 = lax.rsqrt(var2 + EPS)

        def head_block(item):
            block_z, block_b, block_t, block_y = item
            mid_norm = gain2 * (block_z - mean2) * inv2 + shift2
            hidden = prelu_apply(mid_norm, slope3)
            scores = low_back(jnp.dot(low(hidden), head_low, precision=HIGH) + head_bias)
            log_total = jax.nn.logsumexp(scores, axis=1)
            one_hot = (block_y[:, None] == class_ids[None, :]).astype(scores.dtype)
            picked = lax.optimization_barrier(jnp.sum(scores * one_hot, axis=1))
            return (jnp.sum(block_t * (log_total - picked)), scores * block_b[:, None])
        parts, scores_all = lax.map(jax.checkpoint(head_block), (mid_pre, bucket, trained, label_rows))
        return (jnp.sum(parts), scores_all.reshape(NODES, C))
    (loss, logits), back = jax.vjp(forward, features32, w_branch, w_mid, w_head, small_params)
    grads = back((jnp.ones((), loss.dtype), jnp.zeros_like(logits)))
    features_grad, grad_branch, grad_mid, grad_head, grad_small = grads
    root = math.sqrt(NODES)
    mb, ab, nb = nesterov(w_branch, grad_branch, mom_branch, avg_branch, 0.8 / root)
    mm, am, nm = nesterov(w_mid, grad_mid, mom_mid, avg_mid, 0.08 / root)
    mh, ah, nh = nesterov(w_head, grad_head, mom_head, avg_head, 0.3 / root)
    ms, as_small, ns = nesterov(small_params, grad_small, mom_small, avg_small, 1.0 / root)
    return (logits, features_grad, grad_branch, grad_mid, grad_head, grad_small, mb, mm, mh, ms, ab, am, ah, as_small, nb, nm, nh, ns)
```

```python
import functools
import math

import jax
import jax.numpy as jnp
from jax import lax
from jax.experimental import pallas as pl
from jax.experimental.pallas import tpu as pltpu
from jax.sharding import PartitionSpec as P

K = 4
F = 100
H = 512
C = 47


EPS = 1e-05
MOMENTUM = 0.9
DECAY = 0.9


def prelu_apply(values_in, slopes):
    return slopes * values_in + (1.0 - slopes) * jax.nn.softplus(values_in)


def prelu_slope_term(values_in):
    return values_in - jax.nn.softplus(values_in)


def prelu_input_factor(values_in, slopes):
    return slopes + (1.0 - slopes) * jax.nn.sigmoid(values_in)


def split_small(packed):
    width = K * H
    return (
        packed[:width],
        packed[width : 2 * width],
        packed[2 * width : 3 * width],
        packed[3 * width : 4 * width],
        packed[4 * width : 4 * width + H],
        packed[4 * width + H : 4 * width + 2 * H],
        packed[4 * width + 2 * H : 4 * width + 3 * H],
        packed[4 * width + 3 * H :],
    )


def nesterov(weight, gradient, momentum_old, average_old, step_rate):
    momentum_new = MOMENTUM * momentum_old + gradient
    weight_new = weight - step_rate * (gradient + MOMENTUM * momentum_new)
    average_new = DECAY * average_old + (1.0 - DECAY) * weight_new
    return (momentum_new, average_new, weight_new)


def moments(columns_in, bucket):
    masked = columns_in * bucket[:, None]
    totals, count_fill = lax.psum((jnp.sum(masked, axis=0), jnp.sum(bucket)), "shard")
    mean_col = totals / count_fill
    centered = columns_in - mean_col
    squares = lax.psum(jnp.sum(centered * centered * bucket[:, None], axis=0), "shard")
    variance = squares / count_fill
    return (mean_col, lax.rsqrt(variance + EPS), count_fill)


def local(
    features,
    counts,
    labelled,
    labels,
    w_branch,
    w_mid,
    w_head,
    small_params,
    mom_branch,
    mom_mid,
    mom_head,
    mom_small,
    avg_branch,
    avg_mid,
    avg_head,
    avg_small,
):
    node_rows = features.shape[0]
    nodes_all = node_rows * lax.axis_size("shard")
    gain1, shift1, slope1, slope2, gain2, shift2, slope3, head_bias = split_small(small_params)
    slot_index = lax.broadcasted_iota(jnp.int32, (node_rows,), 0)
    bucket = (slot_index < counts[0]).astype(jnp.float32)
    trained = bucket * labelled.astype(jnp.float32)
    branch_low = w_branch.astype(jnp.bfloat16)
    mid_low = w_mid.astype(jnp.bfloat16)
    head_low = w_head.astype(jnp.bfloat16)
    branch_full = lax.all_gather(branch_low, "shard", axis=1, tiled=True)
    feats_three = features.reshape(node_rows, K, F)
    branch_three = branch_full.reshape(K, F, H)
    branch_pre = jnp.einsum(
        "nkf,kfh->nkh", feats_three, branch_three, preferred_element_type=jnp.float32
    ).reshape(node_rows, K * H)
    mean1, inv1, count_fill = moments(branch_pre, bucket)
    branch_hat = (branch_pre - mean1) * inv1
    branch_norm = gain1 * branch_hat + shift1
    branch_act = prelu_apply(branch_norm, slope1)
    concat_low = prelu_apply(branch_act, slope2).astype(jnp.bfloat16)
    mid_full = lax.all_gather(mid_low, "shard", axis=1, tiled=True)
    mid_pre = jnp.dot(concat_low, mid_full, preferred_element_type=jnp.float32)
    mean2, inv2, unused_fill = moments(mid_pre, bucket)
    mid_hat = (mid_pre - mean2) * inv2
    mid_norm = gain2 * mid_hat + shift2
    hidden_low = prelu_apply(mid_norm, slope3).astype(jnp.bfloat16)
    scores = jnp.dot(hidden_low, head_low, preferred_element_type=jnp.float32) + head_bias
    log_total = jax.nn.logsumexp(scores, axis=1)
    prob_rows = jnp.exp(scores - log_total[:, None])
    one_hot = (labels[:, None] == lax.broadcasted_iota(jnp.int32, (1, C), 1)).astype(jnp.float32)
    logit_low = ((prob_rows - one_hot) * trained[:, None]).astype(jnp.bfloat16)
    head_part = jnp.dot(hidden_low.T, logit_low, preferred_element_type=jnp.float32)
    bias_part = jnp.sum(logit_low.astype(jnp.float32), axis=0)
    hidden_grad = jnp.dot(logit_low, head_low.T, preferred_element_type=jnp.float32)
    slope_out_part = jnp.sum(hidden_grad * prelu_slope_term(mid_norm), axis=0)
    mid_norm_grad = hidden_grad * prelu_input_factor(mid_norm, slope3)
    grad_head, grad_bias, grad_slope3, grad_gain2, grad_shift2 = lax.psum(
        (
            head_part,
            bias_part,
            slope_out_part,
            jnp.sum(mid_norm_grad * mid_hat * bucket[:, None], axis=0),
            jnp.sum(mid_norm_grad * bucket[:, None], axis=0),
        ),
        "shard",
    )
    mid_grad_low = (
        gain2
        * inv2
        * bucket[:, None]
        * (mid_norm_grad - (grad_shift2 + mid_hat * grad_gain2) / count_fill)
    ).astype(jnp.bfloat16)
    mid_part = jnp.dot(concat_low.T, mid_grad_low, preferred_element_type=jnp.float32)
    concat_grad = jnp.dot(mid_grad_low, mid_full.T, preferred_element_type=jnp.float32)
    slope_two_part = jnp.sum(concat_grad * prelu_slope_term(branch_act), axis=0)
    act_grad = concat_grad * prelu_input_factor(branch_act, slope2)
    slope_one_part = jnp.sum(act_grad * prelu_slope_term(branch_norm), axis=0)
    norm_grad = act_grad * prelu_input_factor(branch_norm, slope1)
    grad_slope1, grad_slope2, grad_gain1, grad_shift1 = lax.psum(
        (
            slope_one_part,
            slope_two_part,
            jnp.sum(norm_grad * branch_hat * bucket[:, None], axis=0),
            jnp.sum(norm_grad * bucket[:, None], axis=0),
        ),
        "shard",
    )
    branch_grad_low = (
        gain1
        * inv1
        * bucket[:, None]
        * (norm_grad - (grad_shift1 + branch_hat * grad_gain1) / count_fill)
    ).astype(jnp.bfloat16)
    branch_grad_three = branch_grad_low.reshape(node_rows, K, H)
    features_grad = jnp.einsum(
        "nkh,kfh->nkf", branch_grad_three, branch_three, preferred_element_type=jnp.float32
    ).reshape(node_rows, K * F)
    branch_part = jnp.einsum(
        "nkf,nkh->kfh", feats_three, branch_grad_three, preferred_element_type=jnp.float32
    ).reshape(K * F, H)
    grad_branch, grad_mid = (
        lax.psum_scatter(branch_part, "shard", scatter_dimension=1, tiled=True),
        lax.psum_scatter(mid_part, "shard", scatter_dimension=1, tiled=True),
    )
    grad_small = jnp.concatenate(
        [
            grad_gain1,
            grad_shift1,
            grad_slope1,
            grad_slope2,
            grad_gain2,
            grad_shift2,
            grad_slope3,
            grad_bias,
        ]
    )
    root = math.sqrt(nodes_all)
    mom_b, avg_b, new_b = nesterov(w_branch, grad_branch, mom_branch, avg_branch, 0.8 / root)
    mom_m, avg_m, new_m = nesterov(w_mid, grad_mid, mom_mid, avg_mid, 0.08 / root)
    mom_h, avg_h, new_h = nesterov(w_head, grad_head, mom_head, avg_head, 0.3 / root)
    mom_s, avg_s, new_s = nesterov(small_params, grad_small, mom_small, avg_small, 1.0 / root)
    logits = scores * bucket[:, None]
    return (
        logits,
        features_grad,
        grad_branch,
        grad_mid,
        grad_head,
        grad_small,
        mom_b,
        mom_m,
        mom_h,
        mom_s,
        avg_b,
        avg_m,
        avg_h,
        avg_s,
        new_b,
        new_m,
        new_h,
        new_s,
    )


LOG2E = 1.4426950408889634
LN2 = 0.6931471805599453
LOW = jnp.bfloat16
WIDE = jnp.float32
FP = 128
TILE = 256
CHUNK = 32
MESH = pl.DeviceIdType.MESH


def soft_two(u):
    return jnp.maximum(u, jnp.log2(1.0 + jnp.exp2(jnp.minimum(u, 126.0))))


def dot_nn(a, b):
    return jnp.dot(a, b, preferred_element_type=WIDE)


def dot_nt(a, b):
    return lax.dot_general(a, b, (((1,), (1,)), ((), ())), preferred_element_type=WIDE)


def column(row):
    return jnp.broadcast_to(row, (FP, FP)).T


def split_three(v):
    hi = v.astype(LOW)
    rest = v - hi.astype(WIDE)
    mid = rest.astype(LOW)
    return hi, mid, (rest - mid.astype(WIDE)).astype(LOW)


def fold_halves(v):
    return v[:, :128] + v[:, 128:]


def net_kernel(
    nch,
    count_ref,
    feats_hbm,
    code_ref,
    wb_ref,
    wm_ref,
    wh_ref,
    small_ref,
    score_hbm,
    part_hbm,
    soft_hbm,
    gm_out,
    gb_out,
    head_out,
    rows_out,
    corr_out,
    xa,
    cat,
    mid_z,
    dz,
    cat_s,
    soft_s,
    pre_s,
    wp,
    cols,
    wb_own,
    wb_all,
    wm_own,
    wm_all,
    gram,
    gram_sib,
    gram_in,
    gram_all,
    wbt,
    wht,
    whn,
    small_t,
    acc,
    msg_own,
    msg_sib,
    msg_in,
    bn2,
    head_acc,
    bias_acc,
    head_loc,
    head_sib,
    head_in,
    head_all,
    pgrad,
    pgrad_sib,
    pgrad_in,
    gm_in,
    rows_own,
    rows_all,
    part_s,
    score_s,
    load_sem,
    soft_sem,
    part_sem,
    score_sem,
    send_sem,
    recv_sem,
):
    nodes = feats_hbm.shape[1]
    tiles = nodes // TILE
    rb = wb_ref.shape[0]
    hid = H
    me = lax.axis_index("shard")
    chip = me // 2
    core = lax.rem(me, 2)
    sibling = me + 1 - 2 * core
    count = count_ref[0]

    def peer(s):
        return lax.rem(chip + s, nch) * 2 + core

    def origin(s):
        return lax.rem(chip + nch - s, nch)

    def to_peer(i, s, src, dst):
        return pltpu.make_async_remote_copy(
            src_ref=src,
            dst_ref=dst,
            send_sem=send_sem.at[i, s],
            recv_sem=recv_sem.at[i, s],
            device_id=(peer(s),),
            device_id_type=MESH,
        )

    def to_sibling(i, src, dst):
        return pltpu.make_async_remote_copy(
            src_ref=src,
            dst_ref=dst,
            send_sem=send_sem.at[i, 0],
            recv_sem=recv_sem.at[i, 0],
            device_id=(sibling,),
            device_id_type=MESH,
        )

    def mask_row(start, width):
        lane = lax.broadcasted_iota(jnp.int32, (1, width), 1) + start
        return (lane < count).astype(WIDE)

    load = pltpu.make_async_copy(feats_hbm, cat.at[pl.ds(0, K * F), :], load_sem.at[0])
    load.start()

    barrier = pltpu.get_barrier_semaphore()
    for s in range(1, nch):
        pl.semaphore_signal(barrier, inc=1, device_id=(peer(s),), device_id_type=MESH)
    pl.semaphore_signal(barrier, inc=1, device_id=(sibling,), device_id_type=MESH)

    wb_own[...] = jnp.zeros(wb_own.shape, LOW)
    for k in range(K):
        wb_own[k, :, 0:F] = wb_ref[:, k * F : (k + 1) * F].astype(LOW)
    wm_own[...] = wm_ref[...].astype(LOW)
    pl.semaphore_wait(barrier, nch)

    def wb_slot(c):
        return wb_all.at[:, c, core]

    def wb_send(s):
        return to_peer(0, s, wb_own, wb_slot(chip))

    def wm_send(s):
        return to_peer(1, s, wm_own, wm_all.at[chip, core])

    for s in range(1, nch):
        wb_send(s).start()
    wb_all[:, chip, core] = wb_own[...]
    wm_all[chip, core] = wm_own[...]

    small_t[...] = jnp.concatenate(
        [small_ref[...], jnp.zeros((FP - small_ref.shape[0], FP), WIDE)], axis=0
    ).T

    load.wait()
    for s in range(1, nch):
        wm_send(s).start()

    width = 2 * TILE
    row_id = lax.broadcasted_iota(jnp.int32, (112, width), 0)

    def build(i, carry):
        start = pl.multiple_of(i * width, width)
        here = mask_row(start, width)
        x = cat[0 : K * F + 16, pl.ds(start, width)].astype(WIDE)
        for k in range(K):
            piece = x[k * F : k * F + 112]
            piece = jnp.where(row_id < F, piece * here, jnp.where(row_id < F + 3, here, 0.0))
            xa[k, 0:112, pl.ds(start, width)] = piece.astype(LOW)
            xa[k, 112:FP, pl.ds(start, width)] = jnp.zeros((FP - 112, width), LOW)
        return carry

    cat[K * F : K * F + 16, :] = jnp.zeros((16, nodes), LOW)
    lax.fori_loop(0, nodes // width, build, 0)

    rows_g = gram.shape[2]
    for k in range(K):
        g = dot_nt(xa[k], xa[k])
        gram[pl.ds(k * nch // K, nch // K)] = g.reshape(nch // K, 2, rows_g, FP)

    def reduce_one(i, own, sib):
        to_sibling(i, own.at[:, 1 - core], sib).start()
        to_sibling(i, own.at[:, 1 - core], sib).wait()

    def reduce_two(i, own, sib, got):
        own[:, core] = own[:, core] + sib[...]
        for s in range(1, nch):
            to_peer(i, s, own.at[lax.rem(chip + s, nch), core], got.at[chip]).start()
        got[chip] = own[chip, core]

    def reduce_wait(i, own, got):
        for s in range(1, nch):
            to_peer(i, s, own.at[lax.rem(chip + s, nch), core], got.at[chip]).wait_recv()
        for s in range(1, nch):
            to_peer(i, s, own.at[lax.rem(chip + s, nch), core], got.at[chip]).wait_send()

    def total_of(got):
        t = got[0].astype(WIDE)
        for c in range(1, nch):
            t = t + got[c].astype(WIDE)
        return t

    def spread_one(i, every):
        for s in range(1, nch):
            to_peer(i, s, every.at[chip, core], every.at[chip, core]).start()

    def spread_two(i, every):
        for s in range(1, nch):
            to_peer(i, s, every.at[chip, core], every.at[chip, core]).wait()
        to_sibling(i, every.at[:, core], every.at[:, core]).start()

    def spread_wait(i, every):
        to_sibling(i, every.at[:, core], every.at[:, core]).wait()

    reduce_one(2, gram, gram_sib)
    reduce_two(2, gram, gram_sib, gram_in)
    for s in range(1, nch):
        wb_send(s).wait()
    to_sibling(0, wb_all.at[:, :, core], wb_all.at[:, :, core]).start()
    reduce_wait(2, gram, gram_in)
    gram_all[chip, core] = total_of(gram_in)
    spread_one(3, gram_all)
    wht[...] = jnp.zeros(wht.shape, LOW)
    wht[0:C, :] = wh_ref[...].astype(LOW)
    whn[...] = jnp.concatenate(
        [wh_ref[...], jnp.zeros((FP - C, hid), WIDE)], axis=0
    ).T.astype(LOW)
    acc[...] = jnp.zeros(acc.shape, WIDE)
    to_sibling(0, wb_all.at[:, :, core], wb_all.at[:, :, core]).wait()
    for k in range(K):
        wbt[k] = wb_all[k].reshape(hid, FP).astype(WIDE).T.astype(LOW)
    spread_two(3, gram_all)
    spread_wait(3, gram_all)

    def branch_gram(k):
        return gram_all[pl.ds(k * nch // K, nch // K)].reshape(FP, FP)

    def branch_stats(w, g, g_parts):
        filled = g[F : F + 1, F : F + 1]
        wg = dot_nn(w, g_parts[0]) + dot_nn(w, g_parts[1]) + dot_nn(w, g_parts[2])
        wf = w.astype(WIDE)
        mean = wg[:, F : F + 1] / filled
        second = jnp.sum(wg * wf, axis=1, keepdims=True) / filled
        var = jnp.maximum(second - mean * mean, 0.0)
        return wf, wg, mean, lax.rsqrt(var + EPS), filled

    lane = lax.broadcasted_iota(jnp.int32, (FP, FP), 1)
    blocks = hid // FP
    for k in range(K):
        g = branch_gram(k)
        g_parts = split_three(g)
        wk = wb_all[k].reshape(hid, FP)
        for q in range(blocks):
            w = wk[q * FP : (q + 1) * FP]
            wf, wg, mean, inv, filled = branch_stats(w, g, g_parts)
            c = k * blocks + q
            gain = small_t[:, c : c + 1]
            shift = small_t[:, K * blocks + c : K * blocks + c + 1]
            slope1 = small_t[:, 2 * K * blocks + c : 2 * K * blocks + c + 1]
            slope2 = small_t[:, 3 * K * blocks + c : 3 * K * blocks + c + 1]
            ginv = gain * inv
            scaled = wf * (-LOG2E * ginv)
            hi = scaled.astype(LOW).astype(WIDE)
            lo = scaled - hi
            b1, b2, b3 = split_three(-LOG2E * (shift - ginv * mean))
            hi = jnp.where(lane == F, b1.astype(WIDE), hi)
            hi = jnp.where(lane == F + 1, b2.astype(WIDE), hi)
            hi = jnp.where(lane == F + 2, b3.astype(WIDE), hi)
            here = slice(q * FP, (q + 1) * FP)
            wp[k, here, 0:FP] = hi.astype(LOW)
            wp[k, here, FP : 2 * FP] = lo.astype(LOW)
            there = slice(c * FP, (c + 1) * FP)
            cols[0, there, :] = jnp.broadcast_to(1.0 - slope1, (FP, FP))
            cols[1, there, :] = jnp.broadcast_to(1.0 - slope2, (FP, FP))
            cols[2, there, :] = jnp.broadcast_to(ginv, (FP, FP))

    for s in range(1, nch):
        wm_send(s).wait()
    to_sibling(1, wm_all.at[:, core], wm_all.at[:, core]).start()
    to_sibling(1, wm_all.at[:, core], wm_all.at[:, core]).wait()

    def branch_dot(k, j):
        x = xa[k, :, pl.ds(pl.multiple_of(j * TILE, TILE), TILE)]
        pre_s[k % 2] = dot_nn(wp[k], jnp.concatenate([x, x], axis=0))

    def mid_dot(k, slot, start):
        w = wm_all[:, :, :, k * hid : (k + 1) * hid].reshape(hid, hid)
        d = dot_nn(w, cat_s[slot, k * hid : (k + 1) * hid, :])
        if k == 0:
            mid_z[:, pl.ds(start, TILE)] = d
            return
        z = mid_z[:, pl.ds(start, TILE)] + d
        mid_z[:, pl.ds(start, TILE)] = z
        if k == K - 1:
            masked = z * mask_row(start, TILE)
            acc[0] += fold_halves(masked)
            acc[1] += fold_halves(masked * z)

    def forward_chunk(k, r, slot, start):
        rows = slice(k * hid + r, k * hid + r + CHUNK)
        for half in range(2):
            lanes = slice(half * 128, half * 128 + 128)
            u1 = pre_s[k % 2, r : r + CHUNK, lanes]
            m1 = soft_two(u1)
            u2 = u1 - cols[0, rows, :] * m1
            m2 = soft_two(u2)
            v = ((u2 - cols[1, rows, :] * m2) * -LN2).astype(LOW)
            cat_s[slot, rows, lanes] = v
            cat[rows, pl.ds(start + half * 128, 128)] = v
            soft_s[slot, 0, rows, lanes] = m1.astype(LOW)
            soft_s[slot, 1, rows, lanes] = m2.astype(LOW)

    def soft_save(slot, j):
        return pltpu.make_async_copy(soft_s.at[slot], soft_hbm.at[j], soft_sem.at[slot])

    cat_s[1] = jnp.zeros(cat_s.shape[1:], LOW)
    branch_dot(0, 0)

    def forward(i, carry):
        for slot in range(2):
            j = i * 2 + slot

            @pl.when(i > 0)
            def _():
                soft_save(slot, j - 2).wait()

            start = pl.multiple_of(j * TILE, TILE)
            before = pl.multiple_of(jnp.maximum(j - 1, 0) * TILE, TILE)
            for k in range(K):
                mid_dot(k, 1 - slot, before)
                if k < K - 1:
                    branch_dot(k + 1, j)
                else:
                    branch_dot(0, jnp.minimum(j + 1, tiles - 1))
                for r in range(0, hid, CHUNK):
                    forward_chunk(k, r, slot, start)
            soft_save(slot, j).start()
        return carry

    lax.fori_loop(0, tiles // 2, forward, 0)
    for k in range(K):
        mid_dot(k, 1, (tiles - 1) * TILE)
    for slot in range(2):
        soft_save(slot, tiles - 2 + slot).wait()

    def rows_of(i):
        return jnp.sum(acc[i].T, axis=0, keepdims=True)

    def share_start(n, i):
        to_sibling(i, msg_own.at[n], msg_sib.at[n]).start()

    def share_mid(n, i):
        to_sibling(i, msg_own.at[n], msg_sib.at[n]).wait()
        msg_in[n, chip] = msg_own[n] + msg_sib[n]
        for s in range(1, nch):
            to_peer(i, s, msg_in.at[n, chip], msg_in.at[n, chip]).start()

    def share_end(n, i):
        for s in range(1, nch):
            to_peer(i, s, msg_in.at[n, chip], msg_in.at[n, chip]).wait()
        return total_of(msg_in.at[n])

    def put_rows(n, first, row):
        for q in range(blocks):
            msg_own[n, first + q : first + q + 1, :] = row[:, q * FP : (q + 1) * FP]

    put_rows(0, 0, rows_of(0))
    put_rows(0, blocks, rows_of(1))
    share_start(0, 4)
    share_mid(0, 4)
    for r in range(0, K * hid, FP):
        rows = slice(r, r + FP)
        c1 = cols[0, rows, :]
        ginv = cols[2, rows, :]
        cols[0, rows, :] = ginv * (1.0 - c1)
        cols[2, rows, :] = ginv * c1
    for q in range(4):
        w = wm_all[q * nch // 4 : (q + 1) * nch // 4].reshape(FP, 2048)
        w = w.T
        cat_s[q // 2, :, (q % 2) * FP : (q % 2 + 1) * FP] = w
    head_acc[...] = jnp.zeros(head_acc.shape, WIDE)
    bias_acc[...] = jnp.zeros(bias_acc.shape, WIDE)
    acc[...] = jnp.zeros(acc.shape, WIDE)
    tot = share_end(0, 4)
    filled = branch_gram(0)[F : F + 1, F : F + 1]

    base = 4 * K * blocks
    means = []
    for q in range(blocks):
        here = slice(q * FP, (q + 1) * FP)
        gain = small_ref[base + q : base + q + 1, :]
        shift = small_ref[base + blocks + q : base + blocks + q + 1, :]
        slope3 = small_ref[base + 2 * blocks + q : base + 2 * blocks + q + 1, :]
        mean = tot[q : q + 1] / filled
        var = jnp.maximum(tot[blocks + q : blocks + q + 1] / filled - mean * mean, 0.0)
        inv = lax.rsqrt(var + EPS)
        means.append((mean, inv, gain))
        bn2[0, here, :] = column(-LOG2E * gain * inv)
        bn2[1, here, :] = column(-LOG2E * (shift - gain * inv * mean))
        bn2[2, here, :] = column(mean)
        bn2[3, here, :] = column(1.0 - slope3)

    bias_col = small_t[0 : 48, base + 3 * blocks : base + 3 * blocks + 1]
    class_id = lax.broadcasted_iota(jnp.int32, (48, TILE), 0)

    def score_save(slot, j):
        return pltpu.make_async_copy(
            score_s.at[slot],
            score_hbm.at[:, pl.ds(pl.multiple_of(j * TILE, TILE), TILE)],
            score_sem.at[slot],
        )

    def head(i, carry):
        for slot in range(2):
            j = i * 2 + slot

            @pl.when(i > 0)
            def _():
                score_save(slot, j - 2).wait()

            start = pl.multiple_of(j * TILE, TILE)
            here = mask_row(start, TILE)
            for r in range(0, hid, CHUNK):
                rows = slice(r, r + CHUNK)
                for half in range(2):
                    lanes = slice(half * 128, half * 128 + 128)
                    z = mid_z[rows, pl.ds(start + half * 128, 128)]
                    u = z * bn2[0, rows, :] + bn2[1, rows, :]
                    m = soft_two(u)
                    v = (u - bn2[3, rows, :] * m) * -LN2
                    soft_s[0, 0, rows, lanes] = v.astype(LOW)
                    pre_s[0, rows, lanes] = m
            s = dot_nn(wht[...], soft_s[0, 0, 0:hid, :]) + bias_col
            score_s[slot] = s * here
            s = jnp.where(class_id < C, s, -1e30)
            e = jnp.exp(s - jnp.max(s, axis=0, keepdims=True))
            p = e / jnp.sum(e, axis=0, keepdims=True)
            code = code_ref[:, pl.ds(start, TILE)]
            trained = here * (code >= 0).astype(WIDE)
            hot = (class_id == code).astype(WIDE)
            g = ((p - hot) * trained).astype(LOW)
            bias_acc[...] += fold_halves(g.astype(WIDE))
            head_acc[...] += dot_nt(g, soft_s[0, 0, 0:hid, :])
            pre_s[1] = dot_nn(whn[:, 0:48], g)
            for r in range(0, hid, CHUNK):
                rows = slice(r, r + CHUNK)
                sums = [0.0, 0.0, 0.0]
                for half in range(2):
                    lanes = slice(half * 128, half * 128 + 128)
                    d = pre_s[1, rows, lanes]
                    m = pre_s[0, rows, lanes]
                    c3 = bn2[3, rows, :]
                    dy = d * ((1.0 - c3) + c3 * jnp.exp2(-m))
                    z = mid_z[rows, pl.ds(start + half * 128, 128)] - bn2[2, rows, :]
                    sums[0] += d * m
                    sums[1] += dy
                    sums[2] += dy * z
                    dz[rows, pl.ds(start + half * 128, 128)] = dy.astype(LOW)
                for q in range(3):
                    acc[q, rows, :] += sums[q]
            score_save(slot, j).start()
        return carry

    lax.fori_loop(0, tiles // 2, head, 0)
    for slot in range(2):
        score_save(slot, tiles - 2 + slot).wait()

    put_rows(1, 0, rows_of(1))
    put_rows(1, blocks, rows_of(2))
    share_start(1, 5)
    share_mid(1, 5)
    flat = jnp.concatenate(
        [head_acc[:, q * FP : (q + 1) * FP] for q in range(blocks)]
        + [
            jnp.concatenate(
                [bias_acc[...], jnp.zeros((FP - 48, FP), WIDE)], axis=0
            ).T.sum(axis=0, keepdims=True).reshape(1, FP),
            jnp.zeros((7, FP), WIDE),
        ],
        axis=0,
    )
    rows_h = head_loc.shape[2]
    slope_row = rows_of(0) * -LN2
    flat = jnp.concatenate(
        [flat]
        + [slope_row[:, q * FP : (q + 1) * FP] for q in range(blocks)]
        + [jnp.zeros((2 * nch * rows_h - 200 - blocks, FP), WIDE)],
        axis=0,
    )
    head_loc[...] = flat.reshape(nch, 2, rows_h, FP)
    to_sibling(6, head_loc.at[:, 1 - core], head_sib).start()
    tot = share_end(1, 5)

    for q in range(blocks):
        here = slice(q * FP, (q + 1) * FP)
        mean, inv, gain = means[q]
        grad_shift = tot[q : q + 1]
        grad_gain = tot[blocks + q : blocks + q + 1] * inv
        a = gain * inv
        slope = a * grad_gain * inv / filled
        bn2[0, here, :] = column(a)
        bn2[1, here, :] = column(slope)
        bn2[2, here, :] = column(a * grad_shift / filled - slope * mean)
        msg_own[0, q : q + 1, :] = grad_gain
        msg_own[0, blocks + q : blocks + q + 1, :] = grad_shift

    def mid_back(j, carry):
        start = pl.multiple_of(j * TILE, TILE)
        here = mask_row(start, TILE)
        for r in range(0, hid, CHUNK):
            rows = slice(r, r + CHUNK)
            for half in range(2):
                at = pl.ds(start + half * 128, 128)
                d = dz[rows, at].astype(WIDE) * bn2[0, rows, :]
                t = mid_z[rows, at] * bn2[1, rows, :] + bn2[2, rows, :]
                dz[rows, at] = (d - t * here[:, half * 128 : half * 128 + 128]).astype(LOW)
        return carry

    lax.fori_loop(0, tiles, mid_back, 0)

    to_sibling(6, head_loc.at[:, 1 - core], head_sib).wait()
    reduce_two(6, head_loc, head_sib, head_in)

    def mid_grad(i, carry):
        at = pl.multiple_of(i * TILE, TILE)
        mid_z[:, pl.ds(at, TILE)] = dot_nt(dz[...], cat[pl.ds(at, TILE), :])
        return carry

    lax.fori_loop(0, K * hid // TILE, mid_grad, 0)
    width_m = K * hid

    for c in range(nch):
        for e in range(2):
            at = (2 * c + e) * rb

            @pl.when(core != e)
            def _():
                wm_all[c, 0] = mid_z[at : at + rb, 0:width_m].astype(LOW)

    to_sibling(8, wm_all.at[:, 0], wm_all.at[:, 1]).start()
    reduce_wait(6, head_loc, head_in)
    head_all[chip, core] = total_of(head_in)
    spread_one(7, head_all)

    def soft_load(slot, k, j):
        return pltpu.make_async_copy(
            soft_hbm.at[j, :, pl.ds(k * hid, hid), :],
            soft_s.at[slot, :, pl.ds(0, hid), :],
            soft_sem.at[slot],
        )

    def part_save(slot, k, j):
        return pltpu.make_async_copy(
            part_s.at[slot],
            part_hbm.at[k, :, pl.ds(pl.multiple_of(j * TILE, TILE), TILE)],
            part_sem.at[slot],
        )

    def back_dot(k, j, slot):
        w = jnp.concatenate(
            [cat_s[0, k * hid : (k + 1) * hid, :], cat_s[1, k * hid : (k + 1) * hid, :]], axis=1
        )
        pre_s[slot] = dot_nn(w, dz[:, pl.ds(pl.multiple_of(j * TILE, TILE), TILE)])

    def tail_dots(k, j, slot):
        t = soft_s[slot, 0, hid : 2 * hid, :]
        x = xa[k, :, pl.ds(pl.multiple_of(j * TILE, TILE), TILE)]
        acc[2] += dot_nt(t, x)
        part_s[slot] = dot_nn(wbt[k, 0 : part_s.shape[1], :], t).astype(LOW)

    for k in range(K):
        acc[0] = jnp.zeros(acc.shape[1:], WIDE)
        acc[1] = jnp.zeros(acc.shape[1:], WIDE)
        acc[2] = jnp.zeros(acc.shape[1:], WIDE)
        for slot in range(2):
            soft_load(slot, k, slot).start()
        back_dot(k, 0, 0)

        def backward(i, carry):
            for slot in range(2):
                j = i * 2 + slot
                soft_load(slot, k, j).wait()

                @pl.when(i > 0)
                def _():
                    part_save(slot, k, j - 2).wait()

                back_dot(k, jnp.minimum(j + 1, tiles - 1), 1 - slot)
                for r in range(0, hid, CHUNK):
                    rows = slice(r, r + CHUNK)
                    wide_rows = slice(k * hid + r, k * hid + r + CHUNK)
                    sums = [0.0, 0.0]
                    for half in range(2):
                        lanes = slice(half * 128, half * 128 + 128)
                        d = pre_s[slot, rows, lanes]
                        m1 = soft_s[slot, 0, rows, lanes].astype(WIDE)
                        m2 = soft_s[slot, 1, rows, lanes].astype(WIDE)
                        c2 = cols[1, wide_rows, :]
                        da = d * ((1.0 - c2) + c2 * jnp.exp2(-m2))
                        t = da * (cols[0, wide_rows, :] + cols[2, wide_rows, :] * jnp.exp2(-m1))
                        sums[0] += d * m2
                        sums[1] += da * m1
                        soft_s[slot, 0, hid + r : hid + r + CHUNK, lanes] = t.astype(LOW)
                    acc[0, rows, :] += sums[0]
                    acc[1, rows, :] += sums[1]
                tail_dots(k, j, slot)
                part_save(slot, k, j).start()

                @pl.when(i < tiles // 2 - 1)
                def _():
                    soft_load(slot, k, j + 2).start()
            return carry

        lax.fori_loop(0, tiles // 2, backward, 0)
        for slot in range(2):
            part_save(slot, k, tiles - 2 + slot).wait()

        two = lax.broadcasted_iota(jnp.int32, (hid, FP), 1)
        sl2 = jnp.sum(acc[0], axis=1, keepdims=True) * -LN2
        sl1 = jnp.sum(acc[1], axis=1, keepdims=True) * -LN2
        p = jnp.where(two == F + 4, sl1, jnp.where(two == F + 5, sl2, acc[2]))
        if k > 1:
            reduce_wait(9 + k - 2, pgrad.at[k % 2], pgrad_in.at[k - 2])
        pgrad[k % 2] = p.reshape(nch, 2, rb, FP)
        to_sibling(9 + k, pgrad.at[k % 2, :, 1 - core], pgrad_sib.at[k]).start()

        if k == 0:
            to_sibling(8, wm_all.at[:, 0], wm_all.at[:, 1]).wait()
            for c in range(nch):
                for e in range(2):
                    at = (2 * c + e) * rb

                    @pl.when(core == e)
                    def _():
                        v = mid_z[at : at + rb, 0:width_m] + wm_all[c, 1].astype(WIDE)
                        wm_all[c, 0] = v.astype(LOW)

            for s in range(1, nch):
                to_peer(8, s, wm_all.at[lax.rem(chip + s, nch), 0], gm_in.at[chip]).start()
            gm_in[chip] = wm_all[chip, 0]
            spread_two(7, head_all)
        if k == 1:
            spread_wait(7, head_all)
        if k > 0:
            to_sibling(9 + k - 1, pgrad.at[(k - 1) % 2, :, 1 - core], pgrad_sib.at[k - 1]).wait()
            reduce_two(9 + k - 1, pgrad.at[(k - 1) % 2], pgrad_sib.at[k - 1], pgrad_in.at[k - 1])

    k = K - 1
    to_sibling(9 + k, pgrad.at[k % 2, :, 1 - core], pgrad_sib.at[k]).wait()
    reduce_two(9 + k, pgrad.at[k % 2], pgrad_sib.at[k], pgrad_in.at[k])
    for s in range(1, nch):
        to_peer(8, s, wm_all.at[lax.rem(chip + s, nch), 0], gm_in.at[chip]).wait()
    gm_out[...] = total_of(gm_in)
    for k in range(K - 2, K):
        reduce_wait(9 + k, pgrad.at[k % 2], pgrad_in.at[k])

    lane_s = lax.broadcasted_iota(jnp.int32, (rb, FP), 1)
    quant = []
    for k in range(K):
        g = branch_gram(k)
        w = wb_own[k]
        wf, wg, mean, inv, filled = branch_stats(w, g, split_three(g))
        p = total_of(pgrad_in.at[k])
        st = p[:, F : F + 1]
        tz = jnp.sum(jnp.where(lane_s < F, p * wf, 0.0), axis=1, keepdims=True)
        gt = (tz - mean * st) * inv
        totals = g[F : F + 1, :]
        gb_out[k] = p - (st * totals + gt * inv * (wg - mean * totals)) / filled
        q0 = gt * inv / filled
        q1 = st / filled - q0 * mean
        vals = [st, gt, p[:, F + 4 : F + 5], p[:, F + 5 : F + 6], q0, q1, inv]
        block = jnp.zeros((rb, FP), WIDE)
        for n, v in enumerate(vals):
            block = jnp.where(lane_s == n, v, block)
        quant.append(block)
    quant = jnp.concatenate(quant + [jnp.zeros((FP - K * rb, FP), WIDE)], axis=0).T
    rows_own[...] = quant[0:8, :]
    rows_all[chip, core] = rows_own[...]
    spread_one(13, rows_all)
    spread_two(13, rows_all)
    spread_wait(13, rows_all)
    full = []
    per = FP // rb
    lane8 = lax.broadcasted_iota(jnp.int32, (8, FP), 1)
    for k in range(K):
        for t in range(hid // FP):
            v = jnp.zeros((8, FP), WIDE)
            for n in range(per):
                d = t * per + n
                piece = rows_all[d // 2, d % 2]
                moved = pltpu.roll(piece, (n * rb - k * rb) % FP, 1)
                v = jnp.where((lane8 >= n * rb) & (lane8 < (n + 1) * rb), moved, v)
            full.append(v)
    for c in range(K * blocks):
        v = full[c]
        gain = small_ref[c : c + 1, :]
        unit = gain * v[6:7]
        rows_out[c : c + 1, :] = v[1:2] / unit
        rows_out[K * blocks + c : K * blocks + c + 1, :] = v[0:1] / unit
        rows_out[2 * K * blocks + c : 2 * K * blocks + c + 1, :] = v[2:3]
        rows_out[3 * K * blocks + c : 3 * K * blocks + c + 1, :] = v[3:4]
    rows_out[base : base + 2 * blocks, :] = msg_own[0, 0 : 2 * blocks, :]
    head_flat = head_all[...].reshape(2 * nch * rows_h, FP)
    rows_out[base + 2 * blocks : base + 3 * blocks, :] = head_flat[200 : 200 + blocks]
    rows_out[base + 3 * blocks : base + 3 * blocks + 1, :] = head_flat[192:193]
    rows_out[base + 3 * blocks + 1 :, :] = jnp.zeros(
        (rows_out.shape[0] - base - 3 * blocks - 1, FP), WIDE
    )
    for q in range(blocks):
        head_out[:, q * FP : (q + 1) * FP] = head_flat[q * 48 : q * 48 + 48]
    for k in range(K):
        wt = wbt[k].astype(WIDE)
        r0 = jnp.concatenate([full[k * blocks + q][4:5] for q in range(blocks)], axis=1)
        r1 = jnp.concatenate([full[k * blocks + q][5:6] for q in range(blocks)], axis=1)
        m = dot_nn((wt * r0).astype(LOW), wb_all[k].reshape(hid, FP))
        v = jnp.sum(wt * r1, axis=1, keepdims=True)
        corr_out[k] = jnp.where(lane == F, v, m).astype(LOW)


def finish_kernel(count_ref, feats_ref, part_ref, corr_ref, score_ref, grad_ref, logit_ref):
    width = feats_ref.shape[1]
    lane = lax.broadcasted_iota(jnp.int32, (1, width), 1) + pl.program_id(0) * width
    here = (lane < count_ref[0]).astype(WIDE)
    row_id = lax.broadcasted_iota(jnp.int32, (112, width), 0)
    x = feats_ref[...].astype(WIDE)
    x = jnp.concatenate([x, jnp.zeros((16, width), WIDE)], axis=0)
    for k in range(K):
        piece = x[k * F : k * F + 112]
        piece = jnp.where(row_id < F, piece * here, jnp.where(row_id < F + 1, here, 0.0))
        fix = dot_nn(corr_ref[k, 0:112, 0:112], piece.astype(LOW))
        out = part_ref[k].astype(WIDE) - fix
        grad_ref[k * F : (k + 1) * F, :] = out[0:F]
    logit_ref[...] = score_ref[0:C, :]


def fused(
    features,
    counts,
    labelled,
    labels,
    w_branch,
    w_mid,
    w_head,
    small_params,
    mom_branch,
    mom_mid,
    mom_head,
    mom_small,
    avg_branch,
    avg_mid,
    avg_head,
    avg_small,
):
    nodes = features.shape[0]
    devices = lax.axis_size("shard")
    nch = devices // 2
    rb = w_mid.shape[1]
    tiles = nodes // TILE
    rows_g = K * FP // devices
    rows_h = 8
    feats = features.T
    code = jnp.where(labelled > 0, labels, -1).reshape(1, nodes)
    small_rows = -(-small_params.shape[0] // (8 * FP)) * 8
    small = jnp.pad(small_params, (0, small_rows * FP - small_params.shape[0])).reshape(
        small_rows, FP
    )
    vmem = pl.BlockSpec(memory_space=pltpu.VMEM)
    hbm = pl.BlockSpec(memory_space=pl.ANY)
    smem = pl.BlockSpec(memory_space=pltpu.SMEM)
    width_m = K * H
    scores, part, soft, gm, gb, gh, gs, corr = pl.pallas_call(
        functools.partial(net_kernel, nch),
        out_shape=(
            jax.ShapeDtypeStruct((48, nodes), WIDE),
            jax.ShapeDtypeStruct((K, 112, nodes), LOW),
            jax.ShapeDtypeStruct((tiles, 2, width_m, TILE), LOW),
            jax.ShapeDtypeStruct((rb, width_m), WIDE),
            jax.ShapeDtypeStruct((K, rb, FP), WIDE),
            jax.ShapeDtypeStruct((48, H), WIDE),
            jax.ShapeDtypeStruct((small_rows, FP), WIDE),
            jax.ShapeDtypeStruct((K, FP, FP), LOW),
        ),
        in_specs=[smem, hbm] + [vmem] * 5,
        out_specs=(hbm, hbm, hbm, vmem, vmem, vmem, vmem, vmem),
        scratch_shapes=[
            pltpu.VMEM((K, FP, nodes), LOW),
            pltpu.VMEM((width_m, nodes), LOW),
            pltpu.VMEM((H, nodes), WIDE),
            pltpu.VMEM((H, nodes), LOW),
            pltpu.VMEM((2, width_m, TILE), LOW),
            pltpu.VMEM((2, 2, width_m, TILE), LOW),
            pltpu.VMEM((2, H, TILE), WIDE),
            pltpu.VMEM((K, H, 2 * FP), LOW),
            pltpu.VMEM((3, width_m, FP), WIDE),
            pltpu.VMEM((K, rb, FP), LOW),
            pltpu.VMEM((K, nch, 2, rb, FP), LOW),
            pltpu.VMEM((rb, width_m), LOW),
            pltpu.VMEM((nch, 2, rb, width_m), LOW),
            pltpu.VMEM((nch, 2, rows_g, FP), WIDE),
            pltpu.VMEM((nch, rows_g, FP), WIDE),
            pltpu.VMEM((nch, rows_g, FP), WIDE),
            pltpu.VMEM((nch, 2, rows_g, FP), WIDE),
            pltpu.VMEM((K, FP, H), LOW),
            pltpu.VMEM((48, H), LOW),
            pltpu.VMEM((H, FP), LOW),
            pltpu.VMEM((FP, FP), WIDE),
            pltpu.VMEM((3, H, FP), WIDE),
            pltpu.VMEM((2, 8, FP), WIDE),
            pltpu.VMEM((2, 8, FP), WIDE),
            pltpu.VMEM((2, nch, 8, FP), WIDE),
            pltpu.VMEM((4, H, FP), WIDE),
            pltpu.VMEM((48, H), WIDE),
            pltpu.VMEM((48, FP), WIDE),
            pltpu.VMEM((nch, 2, rows_h, FP), WIDE),
            pltpu.VMEM((nch, rows_h, FP), WIDE),
            pltpu.VMEM((nch, rows_h, FP), WIDE),
            pltpu.VMEM((nch, 2, rows_h, FP), WIDE),
            pltpu.VMEM((2, nch, 2, rb, FP), WIDE),
            pltpu.VMEM((K, nch, rb, FP), WIDE),
            pltpu.VMEM((K, nch, rb, FP), WIDE),
            pltpu.VMEM((nch, rb, width_m), LOW),
            pltpu.VMEM((8, FP), WIDE),
            pltpu.VMEM((nch, 2, 8, FP), WIDE),
            pltpu.VMEM((2, 112, TILE), LOW),
            pltpu.VMEM((2, 48, TILE), WIDE),
            pltpu.SemaphoreType.DMA((1,)),
            pltpu.SemaphoreType.DMA((2,)),
            pltpu.SemaphoreType.DMA((2,)),
            pltpu.SemaphoreType.DMA((2,)),
            pltpu.SemaphoreType.DMA((14, nch)),
            pltpu.SemaphoreType.DMA((14, nch)),
        ],
        compiler_params=pltpu.CompilerParams(
            collective_id=0, has_side_effects=True, vmem_limit_bytes=65400 * 1024
        ),
    )(counts, feats, code, w_branch.T, w_mid.T, w_head.T, small)
    step = 512
    fgrad, logits = pl.pallas_call(
        finish_kernel,
        grid=(nodes // step,),
        out_shape=(
            jax.ShapeDtypeStruct((K * F, nodes), WIDE),
            jax.ShapeDtypeStruct((C, nodes), WIDE),
        ),
        in_specs=[
            smem,
            pl.BlockSpec((K * F, step), lambda i: (0, i)),
            pl.BlockSpec((K, 112, step), lambda i: (0, 0, i)),
            pl.BlockSpec((K, FP, FP), lambda i: (0, 0, 0)),
            pl.BlockSpec((48, step), lambda i: (0, i)),
        ],
        out_specs=(
            pl.BlockSpec((K * F, step), lambda i: (0, i)),
            pl.BlockSpec((C, step), lambda i: (0, i)),
        ),
    )(counts, feats, part, corr, scores)
    root = math.sqrt(nodes * devices)
    grad_branch = jnp.concatenate([gb[k, :, :F] for k in range(K)], axis=1).T
    grad_mid = gm.T
    grad_head = gh[:C].T
    grad_small = gs.reshape(-1)[: small_params.shape[0]]
    mom_b, avg_b, new_b = nesterov(w_branch, grad_branch, mom_branch, avg_branch, 0.8 / root)
    mom_m, avg_m, new_m = nesterov(w_mid, grad_mid, mom_mid, avg_mid, 0.08 / root)
    mom_h, avg_h, new_h = nesterov(w_head, grad_head, mom_head, avg_head, 0.3 / root)
    mom_s, avg_s, new_s = nesterov(small_params, grad_small, mom_small, avg_small, 1.0 / root)
    return (
        logits.T,
        fgrad.T,
        grad_branch,
        grad_mid,
        grad_head,
        grad_small,
        mom_b,
        mom_m,
        mom_h,
        mom_s,
        avg_b,
        avg_m,
        avg_h,
        avg_s,
        new_b,
        new_m,
        new_h,
        new_s,
    )


def solution(mesh):
    in_specs = (
        P("shard", None),
        P("shard"),
        P("shard"),
        P("shard"),
        P(None, "shard"),
        P(None, "shard"),
        P(),
        P(),
        P(None, "shard"),
        P(None, "shard"),
        P(),
        P(),
        P(None, "shard"),
        P(None, "shard"),
        P(),
        P(),
    )
    out_specs = (
        P("shard", None),
        P("shard", None),
        P(None, "shard"),
        P(None, "shard"),
        P(),
        P(),
        P(None, "shard"),
        P(None, "shard"),
        P(),
        P(),
        P(None, "shard"),
        P(None, "shard"),
        P(),
        P(),
        P(None, "shard"),
        P(None, "shard"),
        P(),
        P(),
    )
    run = fused if H % (16 * mesh.size) == 0 else local
    return jax.shard_map(run, mesh=mesh, in_specs=in_specs, out_specs=out_specs, check_vma=False)
```

```python
import functools
import math

import jax
import jax.numpy as jnp
from jax import lax
from jax.experimental import pallas as pl
from jax.experimental.pallas import tpu as pltpu
from jax.sharding import PartitionSpec as P

K = 4
F = 100
H = 512
C = 47


EPS = 1e-05
MOMENTUM = 0.9
DECAY = 0.9


def prelu_apply(values_in, slopes):
    return slopes * values_in + (1.0 - slopes) * jax.nn.softplus(values_in)


def prelu_slope_term(values_in):
    return values_in - jax.nn.softplus(values_in)


def prelu_input_factor(values_in, slopes):
    return slopes + (1.0 - slopes) * jax.nn.sigmoid(values_in)


def split_small(packed):
    width = K * H
    return (
        packed[:width],
        packed[width : 2 * width],
        packed[2 * width : 3 * width],
        packed[3 * width : 4 * width],
        packed[4 * width : 4 * width + H],
        packed[4 * width + H : 4 * width + 2 * H],
        packed[4 * width + 2 * H : 4 * width + 3 * H],
        packed[4 * width + 3 * H :],
    )


def nesterov(weight, gradient, momentum_old, average_old, step_rate):
    momentum_new = MOMENTUM * momentum_old + gradient
    weight_new = weight - step_rate * (gradient + MOMENTUM * momentum_new)
    average_new = DECAY * average_old + (1.0 - DECAY) * weight_new
    return (momentum_new, average_new, weight_new)


def moments(columns_in, bucket):
    masked = columns_in * bucket[:, None]
    totals, count_fill = lax.psum((jnp.sum(masked, axis=0), jnp.sum(bucket)), "shard")
    mean_col = totals / count_fill
    centered = columns_in - mean_col
    squares = lax.psum(jnp.sum(centered * centered * bucket[:, None], axis=0), "shard")
    variance = squares / count_fill
    return (mean_col, lax.rsqrt(variance + EPS), count_fill)


def local(
    features,
    counts,
    labelled,
    labels,
    w_branch,
    w_mid,
    w_head,
    small_params,
    mom_branch,
    mom_mid,
    mom_head,
    mom_small,
    avg_branch,
    avg_mid,
    avg_head,
    avg_small,
):
    node_rows = features.shape[0]
    nodes_all = node_rows * lax.axis_size("shard")
    gain1, shift1, slope1, slope2, gain2, shift2, slope3, head_bias = split_small(small_params)
    slot_index = lax.broadcasted_iota(jnp.int32, (node_rows,), 0)
    bucket = (slot_index < counts[0]).astype(jnp.float32)
    trained = bucket * labelled.astype(jnp.float32)
    branch_low = w_branch.astype(jnp.bfloat16)
    mid_low = w_mid.astype(jnp.bfloat16)
    head_low = w_head.astype(jnp.bfloat16)
    branch_full = lax.all_gather(branch_low, "shard", axis=1, tiled=True)
    feats_three = features.reshape(node_rows, K, F)
    branch_three = branch_full.reshape(K, F, H)
    branch_pre = jnp.einsum(
        "nkf,kfh->nkh", feats_three, branch_three, preferred_element_type=jnp.float32
    ).reshape(node_rows, K * H)
    mean1, inv1, count_fill = moments(branch_pre, bucket)
    branch_hat = (branch_pre - mean1) * inv1
    branch_norm = gain1 * branch_hat + shift1
    branch_act = prelu_apply(branch_norm, slope1)
    concat_low = prelu_apply(branch_act, slope2).astype(jnp.bfloat16)
    mid_full = lax.all_gather(mid_low, "shard", axis=1, tiled=True)
    mid_pre = jnp.dot(concat_low, mid_full, preferred_element_type=jnp.float32)
    mean2, inv2, unused_fill = moments(mid_pre, bucket)
    mid_hat = (mid_pre - mean2) * inv2
    mid_norm = gain2 * mid_hat + shift2
    hidden_low = prelu_apply(mid_norm, slope3).astype(jnp.bfloat16)
    scores = jnp.dot(hidden_low, head_low, preferred_element_type=jnp.float32) + head_bias
    log_total = jax.nn.logsumexp(scores, axis=1)
    prob_rows = jnp.exp(scores - log_total[:, None])
    one_hot = (labels[:, None] == lax.broadcasted_iota(jnp.int32, (1, C), 1)).astype(jnp.float32)
    logit_low = ((prob_rows - one_hot) * trained[:, None]).astype(jnp.bfloat16)
    head_part = jnp.dot(hidden_low.T, logit_low, preferred_element_type=jnp.float32)
    bias_part = jnp.sum(logit_low.astype(jnp.float32), axis=0)
    hidden_grad = jnp.dot(logit_low, head_low.T, preferred_element_type=jnp.float32)
    slope_out_part = jnp.sum(hidden_grad * prelu_slope_term(mid_norm), axis=0)
    mid_norm_grad = hidden_grad * prelu_input_factor(mid_norm, slope3)
    grad_head, grad_bias, grad_slope3, grad_gain2, grad_shift2 = lax.psum(
        (
            head_part,
            bias_part,
            slope_out_part,
            jnp.sum(mid_norm_grad * mid_hat * bucket[:, None], axis=0),
            jnp.sum(mid_norm_grad * bucket[:, None], axis=0),
        ),
        "shard",
    )
    mid_grad_low = (
        gain2
        * inv2
        * bucket[:, None]
        * (mid_norm_grad - (grad_shift2 + mid_hat * grad_gain2) / count_fill)
    ).astype(jnp.bfloat16)
    mid_part = jnp.dot(concat_low.T, mid_grad_low, preferred_element_type=jnp.float32)
    concat_grad = jnp.dot(mid_grad_low, mid_full.T, preferred_element_type=jnp.float32)
    slope_two_part = jnp.sum(concat_grad * prelu_slope_term(branch_act), axis=0)
    act_grad = concat_grad * prelu_input_factor(branch_act, slope2)
    slope_one_part = jnp.sum(act_grad * prelu_slope_term(branch_norm), axis=0)
    norm_grad = act_grad * prelu_input_factor(branch_norm, slope1)
    grad_slope1, grad_slope2, grad_gain1, grad_shift1 = lax.psum(
        (
            slope_one_part,
            slope_two_part,
            jnp.sum(norm_grad * branch_hat * bucket[:, None], axis=0),
            jnp.sum(norm_grad * bucket[:, None], axis=0),
        ),
        "shard",
    )
    branch_grad_low = (
        gain1
        * inv1
        * bucket[:, None]
        * (norm_grad - (grad_shift1 + branch_hat * grad_gain1) / count_fill)
    ).astype(jnp.bfloat16)
    branch_grad_three = branch_grad_low.reshape(node_rows, K, H)
    features_grad = jnp.einsum(
        "nkh,kfh->nkf", branch_grad_three, branch_three, preferred_element_type=jnp.float32
    ).reshape(node_rows, K * F)
    branch_part = jnp.einsum(
        "nkf,nkh->kfh", feats_three, branch_grad_three, preferred_element_type=jnp.float32
    ).reshape(K * F, H)
    grad_branch, grad_mid = (
        lax.psum_scatter(branch_part, "shard", scatter_dimension=1, tiled=True),
        lax.psum_scatter(mid_part, "shard", scatter_dimension=1, tiled=True),
    )
    grad_small = jnp.concatenate(
        [
            grad_gain1,
            grad_shift1,
            grad_slope1,
            grad_slope2,
            grad_gain2,
            grad_shift2,
            grad_slope3,
            grad_bias,
        ]
    )
    root = math.sqrt(nodes_all)
    mom_b, avg_b, new_b = nesterov(w_branch, grad_branch, mom_branch, avg_branch, 0.8 / root)
    mom_m, avg_m, new_m = nesterov(w_mid, grad_mid, mom_mid, avg_mid, 0.08 / root)
    mom_h, avg_h, new_h = nesterov(w_head, grad_head, mom_head, avg_head, 0.3 / root)
    mom_s, avg_s, new_s = nesterov(small_params, grad_small, mom_small, avg_small, 1.0 / root)
    logits = scores * bucket[:, None]
    return (
        logits,
        features_grad,
        grad_branch,
        grad_mid,
        grad_head,
        grad_small,
        mom_b,
        mom_m,
        mom_h,
        mom_s,
        avg_b,
        avg_m,
        avg_h,
        avg_s,
        new_b,
        new_m,
        new_h,
        new_s,
    )


LOG2E = 1.4426950408889634
LN2 = 0.6931471805599453
LOW = jnp.bfloat16
WIDE = jnp.float32
FP = 128
TILE = 256
CHUNK = 16
LAG = 8
GROUP = 4
MESH = pl.DeviceIdType.MESH


def soft_two(u):
    return jnp.maximum(u, jnp.log2(1.0 + jnp.exp2(jnp.minimum(u, 126.0))))


def dot_nn(a, b):
    return jnp.dot(a, b, preferred_element_type=WIDE)


def dot_nt(a, b):
    return lax.dot_general(a, b, (((1,), (1,)), ((), ())), preferred_element_type=WIDE)


def column(row):
    return jnp.broadcast_to(row, (FP, FP)).T


def split_three(v):
    hi = v.astype(LOW)
    rest = v - hi.astype(WIDE)
    mid = rest.astype(LOW)
    return hi, mid, (rest - mid.astype(WIDE)).astype(LOW)


def fold_halves(v):
    return v[:, :128] + v[:, 128:]


def net_kernel(
    nch,
    count_ref,
    feats_hbm,
    code_ref,
    wb_ref,
    wm_ref,
    wh_ref,
    small_ref,
    score_hbm,
    part_hbm,
    soft_hbm,
    gm_out,
    gb_out,
    head_out,
    rows_out,
    corr_out,
    xa,
    cat,
    mid_z,
    dz,
    cat_s,
    soft_s,
    pre_s,
    wp,
    cols,
    wb_own,
    wb_all,
    wm_own,
    wm_all,
    gram,
    gram_sib,
    gram_in,
    gram_all,
    wht,
    whn,
    small_t,
    acc,
    msg_own,
    msg_sib,
    msg_in,
    bn2,
    head_acc,
    bias_acc,
    head_loc,
    head_sib,
    head_in,
    head_all,
    pgrad,
    pgrad_sib,
    pgrad_in,
    gm_in,
    rows_own,
    rows_all,
    score_s,
    load_sem,
    soft_sem,
    part_sem,
    score_sem,
    send_sem,
    recv_sem,
):
    nodes = feats_hbm.shape[1]
    tiles = nodes // TILE
    rb = wb_ref.shape[0]
    hid = H
    me = lax.axis_index("shard")
    chip = me // 2
    core = lax.rem(me, 2)
    sibling = me + 1 - 2 * core
    count = count_ref[0]

    def peer(s):
        return lax.rem(chip + s, nch) * 2 + core

    def origin(s):
        return lax.rem(chip + nch - s, nch)

    def to_peer(i, s, src, dst):
        return pltpu.make_async_remote_copy(
            src_ref=src,
            dst_ref=dst,
            send_sem=send_sem.at[i, s],
            recv_sem=recv_sem.at[i, s],
            device_id=(peer(s),),
            device_id_type=MESH,
        )

    def to_sibling(i, src, dst):
        return pltpu.make_async_remote_copy(
            src_ref=src,
            dst_ref=dst,
            send_sem=send_sem.at[i, 0],
            recv_sem=recv_sem.at[i, 0],
            device_id=(sibling,),
            device_id_type=MESH,
        )

    def mask_row(start, width):
        lane = lax.broadcasted_iota(jnp.int32, (1, width), 1) + start
        return (lane < count).astype(WIDE)

    load = pltpu.make_async_copy(feats_hbm, cat.at[pl.ds(0, K * F), :], load_sem.at[0])
    load.start()

    barrier = pltpu.get_barrier_semaphore()
    for s in range(1, nch):
        pl.semaphore_signal(barrier, inc=1, device_id=(peer(s),), device_id_type=MESH)
    pl.semaphore_signal(barrier, inc=1, device_id=(sibling,), device_id_type=MESH)

    wb_own[...] = jnp.zeros(wb_own.shape, LOW)
    for k in range(K):
        wb_own[k, :, 0:F] = wb_ref[:, k * F : (k + 1) * F].astype(LOW)
    wm_own[...] = wm_ref[...].astype(LOW)
    small_t[...] = jnp.concatenate(
        [small_ref[...], jnp.zeros((FP - small_ref.shape[0], FP), WIDE)], axis=0
    ).T
    wht[...] = jnp.zeros(wht.shape, LOW)
    wht[0:C, :] = wh_ref[...].astype(LOW)
    whn[...] = jnp.concatenate(
        [wh_ref[...], jnp.zeros((FP - C, hid), WIDE)], axis=0
    ).T.astype(LOW)
    acc[...] = jnp.zeros(acc.shape, WIDE)
    wb_all[:, chip, core] = wb_own[...]
    wm_all[chip, core] = wm_own[...]

    width = 2 * TILE
    row_id = lax.broadcasted_iota(jnp.int32, (112, width), 0)

    def build(i, carry):
        start = pl.multiple_of(i * width, width)
        here = mask_row(start, width)
        x = cat[0 : K * F + 16, pl.ds(start, width)].astype(WIDE)
        for k in range(K):
            piece = x[k * F : k * F + 112]
            piece = jnp.where(row_id < F, piece * here, jnp.where(row_id < F + 3, here, 0.0))
            xa[k, 0:112, pl.ds(start, width)] = piece.astype(LOW)
            xa[k, 112:FP, pl.ds(start, width)] = jnp.zeros((FP - 112, width), LOW)
        return carry

    load.wait()
    cat[K * F : K * F + 16, :] = jnp.zeros((16, nodes), LOW)
    lax.fori_loop(0, nodes // width, build, 0)

    rows_g = gram.shape[2]
    for k in range(K):
        g = dot_nt(xa[k], xa[k])
        gram[pl.ds(k * nch // K, nch // K)] = g.reshape(nch // K, 2, rows_g, FP)

    def wb_send(s):
        return to_peer(0, s, wb_own, wb_all.at[:, chip, core])

    def wb_pass():
        return to_sibling(0, wb_all.at[:, :, core], wb_all.at[:, :, core])

    def wm_send(s):
        return to_peer(1, s, wm_own, wm_all.at[chip, core])

    def wm_pass():
        return to_sibling(1, wm_all.at[:, core], wm_all.at[:, core])

    pl.semaphore_wait(barrier, nch)

    def reduce_one(i, own, sib):
        to_sibling(i, own.at[:, 1 - core], sib).start()
        to_sibling(i, own.at[:, 1 - core], sib).wait()

    def reduce_two(i, own, sib, got):
        own[:, core] = own[:, core] + sib[...]
        for s in range(1, nch):
            to_peer(i, s, own.at[lax.rem(chip + s, nch), core], got.at[chip]).start()
        got[chip] = own[chip, core]

    def reduce_wait(i, own, got):
        for s in range(1, nch):
            to_peer(i, s, own.at[lax.rem(chip + s, nch), core], got.at[chip]).wait_recv()
        for s in range(1, nch):
            to_peer(i, s, own.at[lax.rem(chip + s, nch), core], got.at[chip]).wait_send()

    def total_of(got):
        t = got[0].astype(WIDE)
        for c in range(1, nch):
            t = t + got[c].astype(WIDE)
        return t

    def spread_one(i, every):
        for s in range(1, nch):
            to_peer(i, s, every.at[chip, core], every.at[chip, core]).start()

    def spread_two(i, every):
        for s in range(1, nch):
            to_peer(i, s, every.at[chip, core], every.at[chip, core]).wait()
        to_sibling(i, every.at[:, core], every.at[:, core]).start()

    def spread_wait(i, every):
        to_sibling(i, every.at[:, core], every.at[:, core]).wait()

    reduce_one(2, gram, gram_sib)
    reduce_two(2, gram, gram_sib, gram_in)
    for s in range(1, nch):
        wb_send(s).start()
    reduce_wait(2, gram, gram_in)
    gram_all[chip, core] = total_of(gram_in)
    spread_one(3, gram_all)
    for s in range(1, nch):
        wb_send(s).wait()
    wb_pass().start()
    for s in range(1, nch):
        wm_send(s).start()
    wb_pass().wait()
    spread_two(3, gram_all)
    spread_wait(3, gram_all)

    def branch_gram(k):
        return gram_all[pl.ds(k * nch // K, nch // K)].reshape(FP, FP)

    def branch_stats(w, g, g_parts):
        filled = g[F : F + 1, F : F + 1]
        wg = dot_nn(w, g_parts[0]) + dot_nn(w, g_parts[1]) + dot_nn(w, g_parts[2])
        wf = w.astype(WIDE)
        mean = wg[:, F : F + 1] / filled
        second = jnp.sum(wg * wf, axis=1, keepdims=True) / filled
        var = jnp.maximum(second - mean * mean, 0.0)
        return wf, wg, mean, lax.rsqrt(var + EPS), filled

    lane = lax.broadcasted_iota(jnp.int32, (FP, FP), 1)
    blocks = hid // FP
    for k in range(K):
        g = branch_gram(k)
        g_parts = split_three(g)
        wk = wb_all[k].reshape(hid, FP)
        for q in range(blocks):
            w = wk[q * FP : (q + 1) * FP]
            wf, wg, mean, inv, filled = branch_stats(w, g, g_parts)
            c = k * blocks + q
            gain = small_t[:, c : c + 1]
            shift = small_t[:, K * blocks + c : K * blocks + c + 1]
            slope1 = small_t[:, 2 * K * blocks + c : 2 * K * blocks + c + 1]
            slope2 = small_t[:, 3 * K * blocks + c : 3 * K * blocks + c + 1]
            ginv = gain * inv
            scaled = wf * (-LOG2E * ginv)
            hi = scaled.astype(LOW).astype(WIDE)
            lo = scaled - hi
            b1, b2, b3 = split_three(-LOG2E * (shift - ginv * mean))
            hi = jnp.where(lane == F, b1.astype(WIDE), hi)
            hi = jnp.where(lane == F + 1, b2.astype(WIDE), hi)
            hi = jnp.where(lane == F + 2, b3.astype(WIDE), hi)
            here = slice(q * FP, (q + 1) * FP)
            wp[k, here, 0:FP] = hi.astype(LOW)
            wp[k, here, FP : 2 * FP] = lo.astype(LOW)
            there = slice(c * FP, (c + 1) * FP)
            cols[0, there, :] = jnp.broadcast_to(1.0 - slope1, (FP, FP))
            cols[1, there, :] = jnp.broadcast_to(1.0 - slope2, (FP, FP))
            cols[2, there, :] = jnp.broadcast_to(ginv, (FP, FP))

    def branch_dot(k, j):
        x = xa[k, :, pl.ds(pl.multiple_of(j * TILE, TILE), TILE)]
        pre_s[k % 2] = dot_nn(wp[k], jnp.concatenate([x, x], axis=0))

    def mid_dot(j):
        at = pl.ds(pl.multiple_of(j * TILE, TILE), TILE)
        mid_z[:, at] = dot_nn(wm_all[...].reshape(hid, K * hid), cat[:, at])
        here = mask_row(j * TILE, TILE)
        for r in range(0, hid, CHUNK):
            rows = slice(r, r + CHUNK)
            z = mid_z[rows, at]
            masked = z * here
            acc[0, rows, :] += fold_halves(masked)
            acc[1, rows, :] += fold_halves(masked * z)

    def forward_chunk(k, j, r, slot):
        rows = slice(r, r + CHUNK)
        wide_rows = slice(k * hid + r, k * hid + r + CHUNK)
        for half in range(2):
            lanes = slice(half * 128, half * 128 + 128)
            u1 = pre_s[k % 2, rows, lanes]
            m1 = soft_two(u1)
            u2 = u1 - cols[0, wide_rows, :] * m1
            m2 = soft_two(u2)
            v = ((u2 - cols[1, wide_rows, :] * m2) * -LN2).astype(LOW)
            cat[wide_rows, pl.ds(pl.multiple_of(j * TILE + half * 128, 128), 128)] = v
            soft_s[slot, 0, k, rows, lanes] = m1.astype(LOW)
            soft_s[slot, 1, k, rows, lanes] = m2.astype(LOW)

    def soft_save(slot, j):
        return pltpu.make_async_copy(soft_s.at[slot], soft_hbm.at[:, j], soft_sem.at[slot])

    def forward(mids):
        def body(i, carry):
            for slot in range(2):
                j = i * 2 + slot
                soft_save(slot, j).wait()
                if mids:
                    mid_dot(j - LAG)
                for k in range(K):
                    if k < K - 1:
                        branch_dot(k + 1, j)
                    else:
                        branch_dot(0, jnp.minimum(j + 1, tiles - 1))
                    for r in range(0, hid, CHUNK):
                        forward_chunk(k, j, r, slot)
                soft_save(slot, j).start()
            return carry

        return body

    for slot in range(2):
        soft_save(slot, slot).start()
    branch_dot(0, 0)
    lax.fori_loop(0, LAG // 2, forward(False), 0)
    for s in range(1, nch):
        wm_send(s).wait()
    wm_pass().start()
    wm_pass().wait()
    lax.fori_loop(LAG // 2, tiles // 2, forward(True), 0)

    def mid_rest(i, carry):
        mid_dot(2 * i)
        mid_dot(2 * i + 1)
        return carry

    lax.fori_loop((tiles - LAG) // 2, tiles // 2, mid_rest, 0)
    for slot in range(2):
        soft_save(slot, tiles - 2 + slot).wait()

    def rows_of(i):
        return jnp.sum(acc[i].T, axis=0, keepdims=True)

    def share_start(n, i):
        to_sibling(i, msg_own.at[n], msg_sib.at[n]).start()

    def share_mid(n, i):
        to_sibling(i, msg_own.at[n], msg_sib.at[n]).wait()
        msg_in[n, chip] = msg_own[n] + msg_sib[n]
        for s in range(1, nch):
            to_peer(i, s, msg_in.at[n, chip], msg_in.at[n, chip]).start()

    def share_end(n, i):
        for s in range(1, nch):
            to_peer(i, s, msg_in.at[n, chip], msg_in.at[n, chip]).wait()
        return total_of(msg_in.at[n])

    def put_rows(n, first, row):
        for q in range(blocks):
            msg_own[n, first + q : first + q + 1, :] = row[:, q * FP : (q + 1) * FP]

    put_rows(0, 0, rows_of(0))
    put_rows(0, blocks, rows_of(1))
    share_start(0, 4)
    share_mid(0, 4)
    for r in range(0, K * hid, FP):
        rows = slice(r, r + FP)
        c1 = cols[0, rows, :]
        ginv = cols[2, rows, :]
        cols[0, rows, :] = ginv * (1.0 - c1)
        cols[2, rows, :] = ginv * c1
    for k in range(K):
        w = wb_all[k].reshape(hid, FP).astype(WIDE).T.astype(LOW)
        wp[2, k * FP : (k + 1) * FP, :] = w[:, 0:TILE]
        wp[3, k * FP : (k + 1) * FP, :] = w[:, TILE : 2 * TILE]
    for q in range(4):
        w = wm_all[q * nch // 4 : (q + 1) * nch // 4].reshape(FP, 2048)
        w = w.T
        cat_s[q // 2, :, (q % 2) * FP : (q % 2 + 1) * FP] = w
    head_acc[...] = jnp.zeros(head_acc.shape, WIDE)
    bias_acc[...] = jnp.zeros(bias_acc.shape, WIDE)
    acc[...] = jnp.zeros(acc.shape, WIDE)
    tot = share_end(0, 4)
    filled = branch_gram(0)[F : F + 1, F : F + 1]

    base = 4 * K * blocks
    means = []
    for q in range(blocks):
        here = slice(q * FP, (q + 1) * FP)
        gain = small_ref[base + q : base + q + 1, :]
        shift = small_ref[base + blocks + q : base + blocks + q + 1, :]
        slope3 = small_ref[base + 2 * blocks + q : base + 2 * blocks + q + 1, :]
        mean = tot[q : q + 1] / filled
        var = jnp.maximum(tot[blocks + q : blocks + q + 1] / filled - mean * mean, 0.0)
        inv = lax.rsqrt(var + EPS)
        means.append((mean, inv, gain))
        bn2[0, here, :] = column(-LOG2E * gain * inv)
        bn2[1, here, :] = column(-LOG2E * (shift - gain * inv * mean))
        bn2[2, here, :] = column(mean)
        bn2[3, here, :] = column(1.0 - slope3)

    bias_col = small_t[0 : 48, base + 3 * blocks : base + 3 * blocks + 1]
    class_id = lax.broadcasted_iota(jnp.int32, (48, TILE), 0)

    def score_save(slot, j):
        return pltpu.make_async_copy(
            score_s.at[slot],
            score_hbm.at[:, pl.ds(pl.multiple_of(j * TILE, TILE), TILE)],
            score_sem.at[slot],
        )

    def head(i, carry):
        for slot in range(2):
            j = i * 2 + slot

            @pl.when(i > 0)
            def _():
                score_save(slot, j - 2).wait()

            start = pl.multiple_of(j * TILE, TILE)
            here = mask_row(start, TILE)
            for r in range(0, hid, CHUNK):
                rows = slice(r, r + CHUNK)
                for half in range(2):
                    lanes = slice(half * 128, half * 128 + 128)
                    z = mid_z[rows, pl.ds(start + half * 128, 128)]
                    u = z * bn2[0, rows, :] + bn2[1, rows, :]
                    m = soft_two(u)
                    v = (u - bn2[3, rows, :] * m) * -LN2
                    soft_s[0, 0, 0, rows, lanes] = v.astype(LOW)
                    pre_s[0, rows, lanes] = m
            s = dot_nn(wht[...], soft_s[0, 0, 0]) + bias_col
            score_s[slot] = s * here
            s = jnp.where(class_id < C, s, -1e30)
            e = jnp.exp(s - jnp.max(s, axis=0, keepdims=True))
            p = e / jnp.sum(e, axis=0, keepdims=True)
            code = code_ref[:, pl.ds(start, TILE)]
            trained = here * (code >= 0).astype(WIDE)
            hot = (class_id == code).astype(WIDE)
            g = ((p - hot) * trained).astype(LOW)
            bias_acc[...] += fold_halves(g.astype(WIDE))
            head_acc[...] += dot_nt(g, soft_s[0, 0, 0])
            pre_s[1] = dot_nn(whn[:, 0:48], g)
            for r in range(0, hid, CHUNK):
                rows = slice(r, r + CHUNK)
                sums = [0.0, 0.0, 0.0]
                for half in range(2):
                    lanes = slice(half * 128, half * 128 + 128)
                    d = pre_s[1, rows, lanes]
                    m = pre_s[0, rows, lanes]
                    c3 = bn2[3, rows, :]
                    dy = d * ((1.0 - c3) + c3 * jnp.exp2(-m))
                    z = mid_z[rows, pl.ds(start + half * 128, 128)] - bn2[2, rows, :]
                    sums[0] += d * m
                    sums[1] += dy
                    sums[2] += dy * z
                    dz[rows, pl.ds(start + half * 128, 128)] = dy.astype(LOW)
                for q in range(3):
                    acc[q, rows, :] += sums[q]
            score_save(slot, j).start()
        return carry

    lax.fori_loop(0, tiles // 2, head, 0)
    for slot in range(2):
        score_save(slot, tiles - 2 + slot).wait()

    put_rows(1, 0, rows_of(1))
    put_rows(1, blocks, rows_of(2))
    share_start(1, 5)
    share_mid(1, 5)
    flat = jnp.concatenate(
        [head_acc[:, q * FP : (q + 1) * FP] for q in range(blocks)]
        + [
            jnp.concatenate(
                [bias_acc[...], jnp.zeros((FP - 48, FP), WIDE)], axis=0
            ).T.sum(axis=0, keepdims=True).reshape(1, FP),
            jnp.zeros((7, FP), WIDE),
        ],
        axis=0,
    )
    rows_h = head_loc.shape[2]
    slope_row = rows_of(0) * -LN2
    flat = jnp.concatenate(
        [flat]
        + [slope_row[:, q * FP : (q + 1) * FP] for q in range(blocks)]
        + [jnp.zeros((2 * nch * rows_h - 200 - blocks, FP), WIDE)],
        axis=0,
    )
    head_loc[...] = flat.reshape(nch, 2, rows_h, FP)
    to_sibling(6, head_loc.at[:, 1 - core], head_sib).start()
    tot = share_end(1, 5)

    for q in range(blocks):
        here = slice(q * FP, (q + 1) * FP)
        mean, inv, gain = means[q]
        grad_shift = tot[q : q + 1]
        grad_gain = tot[blocks + q : blocks + q + 1] * inv
        a = gain * inv
        slope = a * grad_gain * inv / filled
        bn2[0, here, :] = column(a)
        bn2[1, here, :] = column(slope)
        bn2[2, here, :] = column(a * grad_shift / filled - slope * mean)
        msg_own[0, q : q + 1, :] = grad_gain
        msg_own[0, blocks + q : blocks + q + 1, :] = grad_shift

    def mid_back(j, carry):
        start = pl.multiple_of(j * TILE, TILE)
        here = mask_row(start, TILE)
        for r in range(0, hid, CHUNK):
            rows = slice(r, r + CHUNK)
            for half in range(2):
                at = pl.ds(start + half * 128, 128)
                d = dz[rows, at].astype(WIDE) * bn2[0, rows, :]
                t = mid_z[rows, at] * bn2[1, rows, :] + bn2[2, rows, :]
                dz[rows, at] = (d - t * here[:, half * 128 : half * 128 + 128]).astype(LOW)
        return carry

    lax.fori_loop(0, tiles, mid_back, 0)

    to_sibling(6, head_loc.at[:, 1 - core], head_sib).wait()
    reduce_two(6, head_loc, head_sib, head_in)

    width_m = K * hid

    def mid_grad(i, carry):
        at = pl.ds(pl.multiple_of(i * TILE, TILE), TILE)
        pre_s[0] = dot_nt(dz[...], cat[at, :])
        for c in range(nch):
            first = pre_s[0, 2 * c * rb : (2 * c + 1) * rb, :]
            second = pre_s[0, (2 * c + 1) * rb : (2 * c + 2) * rb, :]
            mid_z[c * rb : (c + 1) * rb, at] = jnp.where(core == 0, first, second)
            wm_all[c, 0, :, at] = jnp.where(core == 0, second, first).astype(LOW)
        return carry

    lax.fori_loop(0, width_m // TILE, mid_grad, 0)
    to_sibling(8, wm_all.at[:, 0], wm_all.at[:, 1]).start()
    reduce_wait(6, head_loc, head_in)
    head_all[chip, core] = total_of(head_in)
    spread_one(7, head_all)

    groups = tiles // GROUP

    def soft_load(t):
        k = lax.div(t, groups)
        g = lax.rem(t, groups)
        slot = lax.rem(t, 2)
        return pltpu.make_async_copy(
            soft_hbm.at[:, pl.ds(g * GROUP, GROUP), k], soft_s.at[slot], soft_sem.at[slot]
        )

    def part_save(k):
        return pltpu.make_async_copy(
            cat.at[pl.ds(k * 112, 112), :], part_hbm.at[k], part_sem.at[k]
        )

    def back_dot(k, j, slot, half):
        rows = slice(half * hid // 2, (half + 1) * hid // 2)
        at = slice(k * hid + half * hid // 2, k * hid + (half + 1) * hid // 2)
        w = jnp.concatenate([cat_s[0, at, :], cat_s[1, at, :]], axis=1)
        pre_s[slot, rows, :] = dot_nn(w, dz[:, pl.ds(pl.multiple_of(j * TILE, TILE), TILE)])

    def turned(k):
        rows = slice(k * FP, (k + 1) * FP)
        return jnp.concatenate([wp[2, rows, :], wp[3, rows, :]], axis=1)

    def sum_dot(k, j, slot):
        x = xa[k, :, pl.ds(pl.multiple_of(j * TILE, TILE), TILE)]
        acc[2] += dot_nt(wp[slot], x)

    def part_dot(k, j, slot):
        at = pl.ds(pl.multiple_of(j * TILE, TILE), TILE)
        cat[k * 112 : (k + 1) * 112, at] = dot_nn(turned(k)[0:112], wp[slot]).astype(LOW)

    for t in range(2):
        soft_load(t).start()
    for k in range(K):
        acc[0] = jnp.zeros(acc.shape[1:], WIDE)
        acc[1] = jnp.zeros(acc.shape[1:], WIDE)
        acc[2] = jnp.zeros(acc.shape[1:], WIDE)
        wp[1] = jnp.zeros(wp.shape[1:], LOW)
        back_dot(k, 0, 0, 0)
        back_dot(k, 0, 0, 1)

        def backward(g, carry):
            t = k * groups + g
            side = lax.rem(t, 2)
            soft_load(t).wait()
            for q in range(GROUP):
                j = g * GROUP + q
                slot = q % 2
                after = jnp.minimum(j + 1, tiles - 1)
                before = jnp.maximum(j - 1, 0)
                parts = [
                    functools.partial(back_dot, k, after, 1 - slot, 0),
                    functools.partial(back_dot, k, after, 1 - slot, 1),
                    functools.partial(sum_dot, k, before, 1 - slot),
                    functools.partial(part_dot, k, before, 1 - slot),
                ]
                for n, part in enumerate(parts):
                    part()
                    for r in range(n * hid // 4, (n + 1) * hid // 4, CHUNK):
                        rows = slice(r, r + CHUNK)
                        wide_rows = slice(k * hid + r, k * hid + r + CHUNK)
                        sums = [0.0, 0.0]
                        for half in range(2):
                            lanes = slice(half * 128, half * 128 + 128)
                            d = pre_s[slot, rows, lanes]
                            m1 = soft_s[side, 0, q, rows, lanes].astype(WIDE)
                            m2 = soft_s[side, 1, q, rows, lanes].astype(WIDE)
                            c2 = cols[1, wide_rows, :]
                            da = d * ((1.0 - c2) + c2 * jnp.exp2(-m2))
                            v = da * (
                                cols[0, wide_rows, :] + cols[2, wide_rows, :] * jnp.exp2(-m1)
                            )
                            sums[0] += d * m2
                            sums[1] += da * m1
                            wp[slot, rows, lanes] = v.astype(LOW)
                        acc[0, rows, :] += sums[0]
                        acc[1, rows, :] += sums[1]

            @pl.when(t + 2 < K * groups)
            def _():
                soft_load(t + 2).start()

            return carry

        lax.fori_loop(0, groups, backward, 0)
        sum_dot(k, tiles - 1, 1)
        part_dot(k, tiles - 1, 1)
        part_save(k).start()

        two = lax.broadcasted_iota(jnp.int32, (hid, FP), 1)
        sl2 = jnp.sum(acc[0], axis=1, keepdims=True) * -LN2
        sl1 = jnp.sum(acc[1], axis=1, keepdims=True) * -LN2
        p = jnp.where(two == F + 4, sl1, jnp.where(two == F + 5, sl2, acc[2]))
        if k > 1:
            reduce_wait(9 + k - 2, pgrad.at[k % 2], pgrad_in.at[k - 2])
        pgrad[k % 2] = p.reshape(nch, 2, rb, FP)
        to_sibling(9 + k, pgrad.at[k % 2, :, 1 - core], pgrad_sib.at[k]).start()

        if k == 0:
            to_sibling(8, wm_all.at[:, 0], wm_all.at[:, 1]).wait()
            for c in range(nch):
                v = mid_z[c * rb : (c + 1) * rb, 0:width_m] + wm_all[c, 1].astype(WIDE)
                wm_all[c, 0] = v.astype(LOW)
            for s in range(1, nch):
                to_peer(8, s, wm_all.at[lax.rem(chip + s, nch), 0], gm_in.at[chip]).start()
            gm_in[chip] = wm_all[chip, 0]
            spread_two(7, head_all)
        if k == 1:
            spread_wait(7, head_all)
        if k > 0:
            to_sibling(9 + k - 1, pgrad.at[(k - 1) % 2, :, 1 - core], pgrad_sib.at[k - 1]).wait()
            reduce_two(9 + k - 1, pgrad.at[(k - 1) % 2], pgrad_sib.at[k - 1], pgrad_in.at[k - 1])

    k = K - 1
    to_sibling(9 + k, pgrad.at[k % 2, :, 1 - core], pgrad_sib.at[k]).wait()
    reduce_two(9 + k, pgrad.at[k % 2], pgrad_sib.at[k], pgrad_in.at[k])
    for s in range(1, nch):
        to_peer(8, s, wm_all.at[lax.rem(chip + s, nch), 0], gm_in.at[chip]).wait()
    gm_out[...] = total_of(gm_in)
    for k in range(K - 2, K):
        reduce_wait(9 + k, pgrad.at[k % 2], pgrad_in.at[k])

    for k in range(K):
        part_save(k).wait()

    lane_s = lax.broadcasted_iota(jnp.int32, (rb, FP), 1)
    quant = []
    for k in range(K):
        g = branch_gram(k)
        w = wb_own[k]
        wf, wg, mean, inv, filled = branch_stats(w, g, split_three(g))
        p = total_of(pgrad_in.at[k])
        st = p[:, F : F + 1]
        tz = jnp.sum(jnp.where(lane_s < F, p * wf, 0.0), axis=1, keepdims=True)
        gt = (tz - mean * st) * inv
        totals = g[F : F + 1, :]
        gb_out[k] = p - (st * totals + gt * inv * (wg - mean * totals)) / filled
        q0 = gt * inv / filled
        q1 = st / filled - q0 * mean
        vals = [st, gt, p[:, F + 4 : F + 5], p[:, F + 5 : F + 6], q0, q1, inv]
        block = jnp.zeros((rb, FP), WIDE)
        for n, v in enumerate(vals):
            block = jnp.where(lane_s == n, v, block)
        quant.append(block)
    quant = jnp.concatenate(quant + [jnp.zeros((FP - K * rb, FP), WIDE)], axis=0).T
    rows_own[...] = quant[0:8, :]
    rows_all[chip, core] = rows_own[...]
    spread_one(13, rows_all)
    spread_two(13, rows_all)
    spread_wait(13, rows_all)
    full = []
    per = FP // rb
    lane8 = lax.broadcasted_iota(jnp.int32, (8, FP), 1)
    for k in range(K):
        for t in range(hid // FP):
            v = jnp.zeros((8, FP), WIDE)
            for n in range(per):
                d = t * per + n
                piece = rows_all[d // 2, d % 2]
                moved = pltpu.roll(piece, (n * rb - k * rb) % FP, 1)
                v = jnp.where((lane8 >= n * rb) & (lane8 < (n + 1) * rb), moved, v)
            full.append(v)
    for c in range(K * blocks):
        v = full[c]
        gain = small_ref[c : c + 1, :]
        unit = gain * v[6:7]
        rows_out[c : c + 1, :] = v[1:2] / unit
        rows_out[K * blocks + c : K * blocks + c + 1, :] = v[0:1] / unit
        rows_out[2 * K * blocks + c : 2 * K * blocks + c + 1, :] = v[2:3]
        rows_out[3 * K * blocks + c : 3 * K * blocks + c + 1, :] = v[3:4]
    rows_out[base : base + 2 * blocks, :] = msg_own[0, 0 : 2 * blocks, :]
    head_flat = head_all[...].reshape(2 * nch * rows_h, FP)
    rows_out[base + 2 * blocks : base + 3 * blocks, :] = head_flat[200 : 200 + blocks]
    rows_out[base + 3 * blocks : base + 3 * blocks + 1, :] = head_flat[192:193]
    rows_out[base + 3 * blocks + 1 :, :] = jnp.zeros(
        (rows_out.shape[0] - base - 3 * blocks - 1, FP), WIDE
    )
    for q in range(blocks):
        head_out[:, q * FP : (q + 1) * FP] = head_flat[q * 48 : q * 48 + 48]
    for k in range(K):
        wt = turned(k).astype(WIDE)
        r0 = jnp.concatenate([full[k * blocks + q][4:5] for q in range(blocks)], axis=1)
        r1 = jnp.concatenate([full[k * blocks + q][5:6] for q in range(blocks)], axis=1)
        m = dot_nt((wt * r0).astype(LOW), turned(k))
        v = jnp.sum(wt * r1, axis=1, keepdims=True)
        corr_out[k] = jnp.where(lane == F, v, m).astype(LOW)


def finish_kernel(
    root,
    count_ref,
    feats_ref,
    part_ref,
    corr_ref,
    score_ref,
    gm_ref,
    gb_ref,
    gh_ref,
    *refs,
):
    states, outs = refs[:9], refs[9:]
    grad_ref, logit_ref, grad_b, grad_h = outs[:4]
    new = outs[4:]
    width = feats_ref.shape[1]
    lane = lax.broadcasted_iota(jnp.int32, (1, width), 1) + pl.program_id(0) * width
    here = (lane < count_ref[0]).astype(WIDE)
    row_id = lax.broadcasted_iota(jnp.int32, (112, width), 0)
    x = feats_ref[...].astype(WIDE)
    x = jnp.concatenate([x, jnp.zeros((16, width), WIDE)], axis=0)
    for k in range(K):
        piece = x[k * F : k * F + 112]
        piece = jnp.where(row_id < F, piece * here, jnp.where(row_id < F + 1, here, 0.0))
        fix = dot_nn(corr_ref[k, 0:112, 0:112], piece.astype(LOW))
        out = part_ref[k].astype(WIDE) - fix
        grad_ref[k * F : (k + 1) * F, :] = out[0:F]
    logit_ref[...] = score_ref[0:C, :]

    @pl.when(pl.program_id(0) == 0)
    def _():
        g = jnp.concatenate([gb_ref[k][:, 0:F] for k in range(K)], axis=1)
        grad_b[...] = g
        grad_h[...] = gh_ref[0:C, :]
        for n, (grad, rate) in enumerate(
            ((g, 0.8 / root), (gm_ref[...], 0.08 / root), (gh_ref[0:C, :], 0.3 / root))
        ):
            w, m, a = (r[...] for r in states[3 * n : 3 * n + 3])
            res = nesterov(w, grad, m, a, rate)
            for r, v in zip(new[3 * n : 3 * n + 3], res):
                r[...] = v


def fused(
    features,
    counts,
    labelled,
    labels,
    w_branch,
    w_mid,
    w_head,
    small_params,
    mom_branch,
    mom_mid,
    mom_head,
    mom_small,
    avg_branch,
    avg_mid,
    avg_head,
    avg_small,
):
    nodes = features.shape[0]
    devices = lax.axis_size("shard")
    nch = devices // 2
    rb = w_mid.shape[1]
    tiles = nodes // TILE
    rows_g = K * FP // devices
    rows_h = 8
    feats = features.T
    code = jnp.where(labelled > 0, labels, -1).reshape(1, nodes)
    small_rows = -(-small_params.shape[0] // (8 * FP)) * 8
    small = jnp.pad(small_params, (0, small_rows * FP - small_params.shape[0])).reshape(
        small_rows, FP
    )
    vmem = pl.BlockSpec(memory_space=pltpu.VMEM)
    hbm = pl.BlockSpec(memory_space=pl.ANY)
    smem = pl.BlockSpec(memory_space=pltpu.SMEM)
    width_m = K * H
    scores, part, soft, gm, gb, gh, gs, corr = pl.pallas_call(
        functools.partial(net_kernel, nch),
        out_shape=(
            jax.ShapeDtypeStruct((48, nodes), WIDE),
            jax.ShapeDtypeStruct((K, 112, nodes), LOW),
            jax.ShapeDtypeStruct((2, tiles, K, H, TILE), LOW),
            jax.ShapeDtypeStruct((rb, width_m), WIDE),
            jax.ShapeDtypeStruct((K, rb, FP), WIDE),
            jax.ShapeDtypeStruct((48, H), WIDE),
            jax.ShapeDtypeStruct((small_rows, FP), WIDE),
            jax.ShapeDtypeStruct((K, FP, FP), LOW),
        ),
        in_specs=[smem, hbm] + [vmem] * 5,
        out_specs=(hbm, hbm, hbm, vmem, vmem, vmem, vmem, vmem),
        scratch_shapes=[
            pltpu.VMEM((K, FP, nodes), LOW),
            pltpu.VMEM((width_m, nodes), LOW),
            pltpu.VMEM((H, nodes), WIDE),
            pltpu.VMEM((H, nodes), LOW),
            pltpu.VMEM((2, width_m, TILE), LOW),
            pltpu.VMEM((2, 2, K, H, TILE), LOW),
            pltpu.VMEM((2, H, TILE), WIDE),
            pltpu.VMEM((K, H, 2 * FP), LOW),
            pltpu.VMEM((3, width_m, FP), WIDE),
            pltpu.VMEM((K, rb, FP), LOW),
            pltpu.VMEM((K, nch, 2, rb, FP), LOW),
            pltpu.VMEM((rb, width_m), LOW),
            pltpu.VMEM((nch, 2, rb, width_m), LOW),
            pltpu.VMEM((nch, 2, rows_g, FP), WIDE),
            pltpu.VMEM((nch, rows_g, FP), WIDE),
            pltpu.VMEM((nch, rows_g, FP), WIDE),
            pltpu.VMEM((nch, 2, rows_g, FP), WIDE),
            pltpu.VMEM((48, H), LOW),
            pltpu.VMEM((H, FP), LOW),
            pltpu.VMEM((FP, FP), WIDE),
            pltpu.VMEM((3, H, FP), WIDE),
            pltpu.VMEM((2, 8, FP), WIDE),
            pltpu.VMEM((2, 8, FP), WIDE),
            pltpu.VMEM((2, nch, 8, FP), WIDE),
            pltpu.VMEM((4, H, FP), WIDE),
            pltpu.VMEM((48, H), WIDE),
            pltpu.VMEM((48, FP), WIDE),
            pltpu.VMEM((nch, 2, rows_h, FP), WIDE),
            pltpu.VMEM((nch, rows_h, FP), WIDE),
            pltpu.VMEM((nch, rows_h, FP), WIDE),
            pltpu.VMEM((nch, 2, rows_h, FP), WIDE),
            pltpu.VMEM((2, nch, 2, rb, FP), WIDE),
            pltpu.VMEM((K, nch, rb, FP), WIDE),
            pltpu.VMEM((K, nch, rb, FP), WIDE),
            pltpu.VMEM((nch, rb, width_m), LOW),
            pltpu.VMEM((8, FP), WIDE),
            pltpu.VMEM((nch, 2, 8, FP), WIDE),
            pltpu.VMEM((2, 48, TILE), WIDE),
            pltpu.SemaphoreType.DMA((1,)),
            pltpu.SemaphoreType.DMA((2,)),
            pltpu.SemaphoreType.DMA((K,)),
            pltpu.SemaphoreType.DMA((2,)),
            pltpu.SemaphoreType.DMA((14, nch)),
            pltpu.SemaphoreType.DMA((14, nch)),
        ],
        compiler_params=pltpu.CompilerParams(
            collective_id=0, has_side_effects=True, vmem_limit_bytes=65400 * 1024
        ),
    )(counts, feats, code, w_branch.T, w_mid.T, w_head.T, small)
    step = nodes // 2
    root = math.sqrt(nodes * devices)

    def whole(v):
        return pl.BlockSpec(v.shape, lambda i: (0,) * len(v.shape))

    states = (
        w_branch.T,
        mom_branch.T,
        avg_branch.T,
        w_mid.T,
        mom_mid.T,
        avg_mid.T,
        w_head.T,
        mom_head.T,
        avg_head.T,
    )
    shapes = [jax.ShapeDtypeStruct(v.shape, WIDE) for v in (states[0], states[6]) + states]
    fgrad, logits, grad_b, grad_h, *new = pl.pallas_call(
        functools.partial(finish_kernel, root),
        grid=(nodes // step,),
        out_shape=[
            jax.ShapeDtypeStruct((K * F, nodes), WIDE),
            jax.ShapeDtypeStruct((C, nodes), WIDE),
        ]
        + shapes,
        in_specs=[
            smem,
            pl.BlockSpec((K * F, step), lambda i: (0, i)),
            pl.BlockSpec((K, 112, step), lambda i: (0, 0, i)),
            pl.BlockSpec((K, FP, FP), lambda i: (0, 0, 0)),
            pl.BlockSpec((48, step), lambda i: (0, i)),
        ]
        + [whole(v) for v in (gm, gb, gh) + states],
        out_specs=[
            pl.BlockSpec((K * F, step), lambda i: (0, i)),
            pl.BlockSpec((C, step), lambda i: (0, i)),
        ]
        + [whole(v) for v in shapes],
        compiler_params=pltpu.CompilerParams(vmem_limit_bytes=65400 * 1024),
    )(counts, feats, part, corr, scores, gm, gb, gh, *states)
    grad_small = gs.reshape(-1)[: small_params.shape[0]]
    mom_b, avg_b, new_b, mom_m, avg_m, new_m, mom_h, avg_h, new_h = (v.T for v in new)
    mom_s, avg_s, new_s = nesterov(small_params, grad_small, mom_small, avg_small, 1.0 / root)
    return (
        logits.T,
        fgrad.T,
        grad_b.T,
        gm.T,
        grad_h.T,
        grad_small,
        mom_b,
        mom_m,
        mom_h,
        mom_s,
        avg_b,
        avg_m,
        avg_h,
        avg_s,
        new_b,
        new_m,
        new_h,
        new_s,
    )


def solution(mesh):
    in_specs = (
        P("shard", None),
        P("shard"),
        P("shard"),
        P("shard"),
        P(None, "shard"),
        P(None, "shard"),
        P(),
        P(),
        P(None, "shard"),
        P(None, "shard"),
        P(),
        P(),
        P(None, "shard"),
        P(None, "shard"),
        P(),
        P(),
    )
    out_specs = (
        P("shard", None),
        P("shard", None),
        P(None, "shard"),
        P(None, "shard"),
        P(),
        P(),
        P(None, "shard"),
        P(None, "shard"),
        P(),
        P(),
        P(None, "shard"),
        P(None, "shard"),
        P(),
        P(),
        P(None, "shard"),
        P(None, "shard"),
        P(),
        P(),
    )
    run = fused if H % (16 * mesh.size) == 0 else local
    return jax.shard_map(run, mesh=mesh, in_specs=in_specs, out_specs=out_specs, check_vma=False)
```

```python
import functools
import math

import jax
import jax.numpy as jnp
from jax import lax
from jax.experimental import pallas as pl
from jax.experimental.pallas import tpu as pltpu
from jax.sharding import PartitionSpec as P

K = 4
F = 100
H = 512
C = 47


EPS = 1e-05
MOMENTUM = 0.9
DECAY = 0.9


def prelu_apply(values_in, slopes):
    return slopes * values_in + (1.0 - slopes) * jax.nn.softplus(values_in)


def prelu_slope_term(values_in):
    return values_in - jax.nn.softplus(values_in)


def prelu_input_factor(values_in, slopes):
    return slopes + (1.0 - slopes) * jax.nn.sigmoid(values_in)


def split_small(packed):
    width = K * H
    return (
        packed[:width],
        packed[width : 2 * width],
        packed[2 * width : 3 * width],
        packed[3 * width : 4 * width],
        packed[4 * width : 4 * width + H],
        packed[4 * width + H : 4 * width + 2 * H],
        packed[4 * width + 2 * H : 4 * width + 3 * H],
        packed[4 * width + 3 * H :],
    )


def nesterov(weight, gradient, momentum_old, average_old, step_rate):
    momentum_new = MOMENTUM * momentum_old + gradient
    weight_new = weight - step_rate * (gradient + MOMENTUM * momentum_new)
    average_new = DECAY * average_old + (1.0 - DECAY) * weight_new
    return (momentum_new, average_new, weight_new)


def moments(columns_in, bucket):
    masked = columns_in * bucket[:, None]
    totals, count_fill = lax.psum((jnp.sum(masked, axis=0), jnp.sum(bucket)), "shard")
    mean_col = totals / count_fill
    centered = columns_in - mean_col
    squares = lax.psum(jnp.sum(centered * centered * bucket[:, None], axis=0), "shard")
    variance = squares / count_fill
    return (mean_col, lax.rsqrt(variance + EPS), count_fill)


def local(
    features,
    counts,
    labelled,
    labels,
    w_branch,
    w_mid,
    w_head,
    small_params,
    mom_branch,
    mom_mid,
    mom_head,
    mom_small,
    avg_branch,
    avg_mid,
    avg_head,
    avg_small,
):
    node_rows = features.shape[0]
    nodes_all = node_rows * lax.axis_size("shard")
    gain1, shift1, slope1, slope2, gain2, shift2, slope3, head_bias = split_small(small_params)
    slot_index = lax.broadcasted_iota(jnp.int32, (node_rows,), 0)
    bucket = (slot_index < counts[0]).astype(jnp.float32)
    trained = bucket * labelled.astype(jnp.float32)
    branch_low = w_branch.astype(jnp.bfloat16)
    mid_low = w_mid.astype(jnp.bfloat16)
    head_low = w_head.astype(jnp.bfloat16)
    branch_full = lax.all_gather(branch_low, "shard", axis=1, tiled=True)
    feats_three = features.reshape(node_rows, K, F)
    branch_three = branch_full.reshape(K, F, H)
    branch_pre = jnp.einsum(
        "nkf,kfh->nkh", feats_three, branch_three, preferred_element_type=jnp.float32
    ).reshape(node_rows, K * H)
    mean1, inv1, count_fill = moments(branch_pre, bucket)
    branch_hat = (branch_pre - mean1) * inv1
    branch_norm = gain1 * branch_hat + shift1
    branch_act = prelu_apply(branch_norm, slope1)
    concat_low = prelu_apply(branch_act, slope2).astype(jnp.bfloat16)
    mid_full = lax.all_gather(mid_low, "shard", axis=1, tiled=True)
    mid_pre = jnp.dot(concat_low, mid_full, preferred_element_type=jnp.float32)
    mean2, inv2, unused_fill = moments(mid_pre, bucket)
    mid_hat = (mid_pre - mean2) * inv2
    mid_norm = gain2 * mid_hat + shift2
    hidden_low = prelu_apply(mid_norm, slope3).astype(jnp.bfloat16)
    scores = jnp.dot(hidden_low, head_low, preferred_element_type=jnp.float32) + head_bias
    log_total = jax.nn.logsumexp(scores, axis=1)
    prob_rows = jnp.exp(scores - log_total[:, None])
    one_hot = (labels[:, None] == lax.broadcasted_iota(jnp.int32, (1, C), 1)).astype(jnp.float32)
    logit_low = ((prob_rows - one_hot) * trained[:, None]).astype(jnp.bfloat16)
    head_part = jnp.dot(hidden_low.T, logit_low, preferred_element_type=jnp.float32)
    bias_part = jnp.sum(logit_low.astype(jnp.float32), axis=0)
    hidden_grad = jnp.dot(logit_low, head_low.T, preferred_element_type=jnp.float32)
    slope_out_part = jnp.sum(hidden_grad * prelu_slope_term(mid_norm), axis=0)
    mid_norm_grad = hidden_grad * prelu_input_factor(mid_norm, slope3)
    grad_head, grad_bias, grad_slope3, grad_gain2, grad_shift2 = lax.psum(
        (
            head_part,
            bias_part,
            slope_out_part,
            jnp.sum(mid_norm_grad * mid_hat * bucket[:, None], axis=0),
            jnp.sum(mid_norm_grad * bucket[:, None], axis=0),
        ),
        "shard",
    )
    mid_grad_low = (
        gain2
        * inv2
        * bucket[:, None]
        * (mid_norm_grad - (grad_shift2 + mid_hat * grad_gain2) / count_fill)
    ).astype(jnp.bfloat16)
    mid_part = jnp.dot(concat_low.T, mid_grad_low, preferred_element_type=jnp.float32)
    concat_grad = jnp.dot(mid_grad_low, mid_full.T, preferred_element_type=jnp.float32)
    slope_two_part = jnp.sum(concat_grad * prelu_slope_term(branch_act), axis=0)
    act_grad = concat_grad * prelu_input_factor(branch_act, slope2)
    slope_one_part = jnp.sum(act_grad * prelu_slope_term(branch_norm), axis=0)
    norm_grad = act_grad * prelu_input_factor(branch_norm, slope1)
    grad_slope1, grad_slope2, grad_gain1, grad_shift1 = lax.psum(
        (
            slope_one_part,
            slope_two_part,
            jnp.sum(norm_grad * branch_hat * bucket[:, None], axis=0),
            jnp.sum(norm_grad * bucket[:, None], axis=0),
        ),
        "shard",
    )
    branch_grad_low = (
        gain1
        * inv1
        * bucket[:, None]
        * (norm_grad - (grad_shift1 + branch_hat * grad_gain1) / count_fill)
    ).astype(jnp.bfloat16)
    branch_grad_three = branch_grad_low.reshape(node_rows, K, H)
    features_grad = jnp.einsum(
        "nkh,kfh->nkf", branch_grad_three, branch_three, preferred_element_type=jnp.float32
    ).reshape(node_rows, K * F)
    branch_part = jnp.einsum(
        "nkf,nkh->kfh", feats_three, branch_grad_three, preferred_element_type=jnp.float32
    ).reshape(K * F, H)
    grad_branch, grad_mid = (
        lax.psum_scatter(branch_part, "shard", scatter_dimension=1, tiled=True),
        lax.psum_scatter(mid_part, "shard", scatter_dimension=1, tiled=True),
    )
    grad_small = jnp.concatenate(
        [
            grad_gain1,
            grad_shift1,
            grad_slope1,
            grad_slope2,
            grad_gain2,
            grad_shift2,
            grad_slope3,
            grad_bias,
        ]
    )
    root = math.sqrt(nodes_all)
    mom_b, avg_b, new_b = nesterov(w_branch, grad_branch, mom_branch, avg_branch, 0.8 / root)
    mom_m, avg_m, new_m = nesterov(w_mid, grad_mid, mom_mid, avg_mid, 0.08 / root)
    mom_h, avg_h, new_h = nesterov(w_head, grad_head, mom_head, avg_head, 0.3 / root)
    mom_s, avg_s, new_s = nesterov(small_params, grad_small, mom_small, avg_small, 1.0 / root)
    logits = scores * bucket[:, None]
    return (
        logits,
        features_grad,
        grad_branch,
        grad_mid,
        grad_head,
        grad_small,
        mom_b,
        mom_m,
        mom_h,
        mom_s,
        avg_b,
        avg_m,
        avg_h,
        avg_s,
        new_b,
        new_m,
        new_h,
        new_s,
    )


LOG2E = 1.4426950408889634
LN2 = 0.6931471805599453
LOW = jnp.bfloat16
WIDE = jnp.float32
FP = 128
TILE = 256
CHUNK = 16
LAG = 10
GROUP = 4
MESH = pl.DeviceIdType.MESH


def soft_two(u):
    return jnp.maximum(u, jnp.log2(1.0 + jnp.exp2(jnp.minimum(u, 126.0))))


def dot_nn(a, b):
    return jnp.dot(a, b, preferred_element_type=WIDE)


def dot_nt(a, b):
    return lax.dot_general(a, b, (((1,), (1,)), ((), ())), preferred_element_type=WIDE)


def column(row):
    return jnp.broadcast_to(row, (FP, FP)).T


def split_three(v):
    hi = v.astype(LOW)
    rest = v - hi.astype(WIDE)
    mid = rest.astype(LOW)
    return hi, mid, (rest - mid.astype(WIDE)).astype(LOW)


def fold_halves(v):
    return v[:, :128] + v[:, 128:]


def net_kernel(
    nch,
    count_ref,
    feats_hbm,
    label_ref,
    marked_ref,
    wb_ref,
    wm_ref,
    wh_ref,
    small_ref,
    score_hbm,
    part_hbm,
    soft_hbm,
    gm_out,
    gb_out,
    head_out,
    rows_out,
    corr_out,
    xa,
    cat,
    mid_z,
    dz,
    cat_s,
    soft_s,
    pre_s,
    wp,
    cols,
    wb_own,
    wb_all,
    wm_own,
    wm_all,
    gram,
    gram_sib,
    gram_in,
    gram_all,
    wht,
    whn,
    small_t,
    acc,
    msg_own,
    msg_sib,
    msg_in,
    bn2,
    head_acc,
    bias_acc,
    head_loc,
    head_sib,
    head_in,
    head_all,
    pgrad,
    pgrad_sib,
    pgrad_in,
    gm_in,
    rows_own,
    rows_all,
    score_s,
    load_sem,
    soft_sem,
    part_sem,
    score_sem,
    send_sem,
    recv_sem,
):
    nodes = feats_hbm.shape[1]
    tiles = nodes // TILE
    rb = wb_ref.shape[0]
    hid = H
    me = lax.axis_index("shard")
    chip = me // 2
    core = lax.rem(me, 2)
    sibling = me + 1 - 2 * core
    count = count_ref[0]

    def peer(s):
        return lax.rem(chip + s, nch) * 2 + core

    def origin(s):
        return lax.rem(chip + nch - s, nch)

    def to_peer(i, s, src, dst):
        return pltpu.make_async_remote_copy(
            src_ref=src,
            dst_ref=dst,
            send_sem=send_sem.at[i, s],
            recv_sem=recv_sem.at[i, s],
            device_id=(peer(s),),
            device_id_type=MESH,
        )

    def to_sibling(i, src, dst):
        return pltpu.make_async_remote_copy(
            src_ref=src,
            dst_ref=dst,
            send_sem=send_sem.at[i, 0],
            recv_sem=recv_sem.at[i, 0],
            device_id=(sibling,),
            device_id_type=MESH,
        )

    def mask_row(start, width):
        lane = lax.broadcasted_iota(jnp.int32, (1, width), 1) + start
        return (lane < count).astype(WIDE)

    load = pltpu.make_async_copy(feats_hbm, cat.at[pl.ds(0, K * F), :], load_sem.at[0])
    load.start()

    barrier = pltpu.get_barrier_semaphore()
    for s in range(1, nch):
        pl.semaphore_signal(barrier, inc=1, device_id=(peer(s),), device_id_type=MESH)
    pl.semaphore_signal(barrier, inc=1, device_id=(sibling,), device_id_type=MESH)

    width = 2 * TILE
    row_id = lax.broadcasted_iota(jnp.int32, (112, width), 0)

    def build(i, carry):
        start = pl.multiple_of(i * width, width)
        here = mask_row(start, width)
        x = cat[0 : K * F + 16, pl.ds(start, width)].astype(WIDE)
        for k in range(K):
            piece = x[k * F : k * F + 112]
            piece = jnp.where(row_id < F, piece * here, jnp.where(row_id < F + 3, here, 0.0))
            xa[k, 0:112, pl.ds(start, width)] = piece.astype(LOW)
            xa[k, 112:FP, pl.ds(start, width)] = jnp.zeros((FP - 112, width), LOW)
        return carry

    load.wait()
    cat[K * F : K * F + 16, :] = jnp.zeros((16, nodes), LOW)
    lax.fori_loop(0, nodes // width, build, 0)

    rows_g = gram.shape[2]
    for k in range(K):
        g = dot_nt(xa[k], xa[k])
        gram[pl.ds(k * nch // K, nch // K)] = g.reshape(nch // K, 2, rows_g, FP)

    def wb_send(s):
        return to_peer(0, s, wb_own, wb_all.at[:, chip, core])

    def wb_pass():
        return to_sibling(0, wb_all.at[:, :, core], wb_all.at[:, :, core])

    def wm_send(s):
        return to_peer(1, s, wm_own, wm_all.at[chip, core])

    def wm_pass():
        return to_sibling(1, wm_all.at[:, core], wm_all.at[:, core])

    pl.semaphore_wait(barrier, nch)

    def reduce_two(i, own, sib, got):
        own[:, core] = own[:, core] + sib[...]
        for s in range(1, nch):
            to_peer(i, s, own.at[lax.rem(chip + s, nch), core], got.at[chip]).start()
        got[chip] = own[chip, core]

    def reduce_wait(i, own, got):
        for s in range(1, nch):
            to_peer(i, s, own.at[lax.rem(chip + s, nch), core], got.at[chip]).wait_recv()
        for s in range(1, nch):
            to_peer(i, s, own.at[lax.rem(chip + s, nch), core], got.at[chip]).wait_send()

    def total_of(got):
        t = got[0].astype(WIDE)
        for c in range(1, nch):
            t = t + got[c].astype(WIDE)
        return t

    def spread_one(i, every):
        for s in range(1, nch):
            to_peer(i, s, every.at[chip, core], every.at[chip, core]).start()

    def spread_two(i, every):
        for s in range(1, nch):
            to_peer(i, s, every.at[chip, core], every.at[chip, core]).wait()
        to_sibling(i, every.at[:, core], every.at[:, core]).start()

    def spread_wait(i, every):
        to_sibling(i, every.at[:, core], every.at[:, core]).wait()

    to_sibling(2, gram.at[:, 1 - core], gram_sib).start()
    wb_own[...] = jnp.zeros(wb_own.shape, LOW)
    for k in range(K):
        wb_own[k, :, 0:F] = wb_ref[:, k * F : (k + 1) * F].astype(LOW)
    wb_all[:, chip, core] = wb_own[...]
    to_sibling(2, gram.at[:, 1 - core], gram_sib).wait()
    reduce_two(2, gram, gram_sib, gram_in)
    for s in range(1, nch):
        wb_send(s).start()
    small_t[...] = jnp.concatenate(
        [small_ref[...], jnp.zeros((FP - small_ref.shape[0], FP), WIDE)], axis=0
    ).T
    wht[...] = jnp.zeros(wht.shape, LOW)
    wht[0:C, :] = wh_ref[...].astype(LOW)
    whn[...] = jnp.concatenate(
        [wh_ref[...], jnp.zeros((FP - C, hid), WIDE)], axis=0
    ).T.astype(LOW)
    acc[...] = jnp.zeros(acc.shape, WIDE)
    wm_own[...] = wm_ref[...].astype(LOW)
    wm_all[chip, core] = wm_own[...]

    reduce_wait(2, gram, gram_in)
    gram_all[chip, core] = total_of(gram_in)
    spread_one(3, gram_all)
    for s in range(1, nch):
        wb_send(s).wait()
    wb_pass().start()
    for s in range(1, nch):
        wm_send(s).start()
    wb_pass().wait()
    spread_two(3, gram_all)
    spread_wait(3, gram_all)

    def branch_gram(k):
        return gram_all[pl.ds(k * nch // K, nch // K)].reshape(FP, FP)

    def branch_stats(w, g, g_parts):
        filled = g[F : F + 1, F : F + 1]
        wg = dot_nn(w, g_parts[0]) + dot_nn(w, g_parts[1]) + dot_nn(w, g_parts[2])
        wf = w.astype(WIDE)
        mean = wg[:, F : F + 1] / filled
        second = jnp.sum(wg * wf, axis=1, keepdims=True) / filled
        var = jnp.maximum(second - mean * mean, 0.0)
        return wf, wg, mean, lax.rsqrt(var + EPS), filled

    lane = lax.broadcasted_iota(jnp.int32, (FP, FP), 1)
    blocks = hid // FP
    for k in range(K):
        g = branch_gram(k)
        g_parts = split_three(g)
        wk = wb_all[k].reshape(hid, FP)
        for q in range(blocks):
            w = wk[q * FP : (q + 1) * FP]
            wf, wg, mean, inv, filled = branch_stats(w, g, g_parts)
            c = k * blocks + q
            gain = small_t[:, c : c + 1]
            shift = small_t[:, K * blocks + c : K * blocks + c + 1]
            slope1 = small_t[:, 2 * K * blocks + c : 2 * K * blocks + c + 1]
            slope2 = small_t[:, 3 * K * blocks + c : 3 * K * blocks + c + 1]
            ginv = gain * inv
            scaled = wf * (-LOG2E * ginv)
            hi = scaled.astype(LOW).astype(WIDE)
            lo = scaled - hi
            b1, b2, b3 = split_three(-LOG2E * (shift - ginv * mean))
            hi = jnp.where(lane == F, b1.astype(WIDE), hi)
            hi = jnp.where(lane == F + 1, b2.astype(WIDE), hi)
            hi = jnp.where(lane == F + 2, b3.astype(WIDE), hi)
            here = slice(q * FP, (q + 1) * FP)
            wp[k, here, 0:FP] = hi.astype(LOW)
            wp[k, here, FP : 2 * FP] = lo.astype(LOW)
            there = slice(c * FP, (c + 1) * FP)
            cols[0, there, :] = jnp.broadcast_to(1.0 - slope1, (FP, FP))
            cols[1, there, :] = jnp.broadcast_to(1.0 - slope2, (FP, FP))
            cols[2, there, :] = jnp.broadcast_to(ginv, (FP, FP))

    def branch_dot(k, j):
        x = xa[k, :, pl.ds(pl.multiple_of(j * TILE, TILE), TILE)]
        pre_s[k % 2] = dot_nn(wp[k], jnp.concatenate([x, x], axis=0))

    def mid_dot(j):
        at = pl.ds(pl.multiple_of(j * TILE, TILE), TILE)
        mid_z[:, at] = dot_nn(wm_all[...].reshape(hid, K * hid), cat[:, at])
        here = mask_row(j * TILE, TILE)
        for r in range(0, hid, CHUNK):
            rows = slice(r, r + CHUNK)
            z = mid_z[rows, at]
            masked = z * here
            acc[0, rows, :] += fold_halves(masked)
            acc[1, rows, :] += fold_halves(masked * z)

    def forward_chunk(k, j, r, slot):
        rows = slice(r, r + CHUNK)
        wide_rows = slice(k * hid + r, k * hid + r + CHUNK)
        for half in range(2):
            lanes = slice(half * 128, half * 128 + 128)
            u1 = pre_s[k % 2, rows, lanes]
            m1 = soft_two(u1)
            u2 = u1 - cols[0, wide_rows, :] * m1
            m2 = soft_two(u2)
            v = ((u2 - cols[1, wide_rows, :] * m2) * -LN2).astype(LOW)
            cat[wide_rows, pl.ds(pl.multiple_of(j * TILE + half * 128, 128), 128)] = v
            soft_s[slot, 0, k, rows, lanes] = m1.astype(LOW)
            soft_s[slot, 1, k, rows, lanes] = m2.astype(LOW)

    def soft_save(slot, j):
        return pltpu.make_async_copy(soft_s.at[slot], soft_hbm.at[:, j], soft_sem.at[slot])

    def forward(mids):
        def body(i, carry):
            for slot in range(2):
                j = i * 2 + slot
                soft_save(slot, j).wait()
                if mids:
                    mid_dot(j - LAG)
                for k in range(K):
                    if k < K - 1:
                        branch_dot(k + 1, j)
                    else:
                        branch_dot(0, jnp.minimum(j + 1, tiles - 1))
                    for r in range(0, hid, CHUNK):
                        forward_chunk(k, j, r, slot)
                soft_save(slot, j).start()
            return carry

        return body

    for slot in range(2):
        soft_save(slot, slot).start()
    branch_dot(0, 0)
    lax.fori_loop(0, LAG // 2, forward(False), 0)
    for s in range(1, nch):
        wm_send(s).wait()
    wm_pass().start()
    wm_pass().wait()
    lax.fori_loop(LAG // 2, tiles // 2, forward(True), 0)

    def mid_rest(i, carry):
        mid_dot(2 * i)
        mid_dot(2 * i + 1)
        return carry

    lax.fori_loop((tiles - LAG) // 2, tiles // 2, mid_rest, 0)
    for slot in range(2):
        soft_save(slot, tiles - 2 + slot).wait()

    def rows_of(i):
        return jnp.sum(acc[i].T, axis=0, keepdims=True)

    def share_start(n, i):
        to_sibling(i, msg_own.at[n], msg_sib.at[n]).start()

    def share_mid(n, i):
        to_sibling(i, msg_own.at[n], msg_sib.at[n]).wait()
        msg_in[n, chip] = msg_own[n] + msg_sib[n]
        for s in range(1, nch):
            to_peer(i, s, msg_in.at[n, chip], msg_in.at[n, chip]).start()

    def share_end(n, i):
        for s in range(1, nch):
            to_peer(i, s, msg_in.at[n, chip], msg_in.at[n, chip]).wait()
        return total_of(msg_in.at[n])

    def put_rows(n, first, row):
        for q in range(blocks):
            msg_own[n, first + q : first + q + 1, :] = row[:, q * FP : (q + 1) * FP]

    put_rows(0, 0, rows_of(0))
    put_rows(0, blocks, rows_of(1))
    share_start(0, 4)
    share_mid(0, 4)
    for r in range(0, K * hid, FP):
        rows = slice(r, r + FP)
        c1 = cols[0, rows, :]
        ginv = cols[2, rows, :]
        cols[0, rows, :] = ginv * (1.0 - c1)
        cols[2, rows, :] = ginv * c1
    for k in range(K):
        w = wb_all[k].reshape(hid, FP).astype(WIDE).T.astype(LOW)
        wp[2, k * FP : (k + 1) * FP, :] = w[:, 0:TILE]
        wp[3, k * FP : (k + 1) * FP, :] = w[:, TILE : 2 * TILE]
    for q in range(4):
        w = wm_all[q * nch // 4 : (q + 1) * nch // 4].reshape(FP, 2048)
        w = w.T
        cat_s[q // 2, :, (q % 2) * FP : (q % 2 + 1) * FP] = w
    head_acc[...] = jnp.zeros(head_acc.shape, WIDE)
    bias_acc[...] = jnp.zeros(bias_acc.shape, WIDE)
    acc[...] = jnp.zeros(acc.shape, WIDE)
    tot = share_end(0, 4)
    filled = branch_gram(0)[F : F + 1, F : F + 1]

    base = 4 * K * blocks
    means = []
    for q in range(blocks):
        here = slice(q * FP, (q + 1) * FP)
        gain = small_ref[base + q : base + q + 1, :]
        shift = small_ref[base + blocks + q : base + blocks + q + 1, :]
        slope3 = small_ref[base + 2 * blocks + q : base + 2 * blocks + q + 1, :]
        mean = tot[q : q + 1] / filled
        var = jnp.maximum(tot[blocks + q : blocks + q + 1] / filled - mean * mean, 0.0)
        inv = lax.rsqrt(var + EPS)
        means.append((mean, inv, gain))
        bn2[0, here, :] = column(-LOG2E * gain * inv)
        bn2[1, here, :] = column(-LOG2E * (shift - gain * inv * mean))
        bn2[2, here, :] = column(mean)
        bn2[3, here, :] = column(1.0 - slope3)

    bias_col = small_t[0 : 48, base + 3 * blocks : base + 3 * blocks + 1]
    class_id = lax.broadcasted_iota(jnp.int32, (48, TILE), 0)

    def score_save(slot, j):
        return pltpu.make_async_copy(
            score_s.at[slot],
            score_hbm.at[:, pl.ds(pl.multiple_of(j * TILE, TILE), TILE)],
            score_sem.at[slot],
        )

    def head(i, carry):
        @pl.when(i > 0)
        def _():
            for slot in range(2):
                score_save(slot, 2 * i - 2 + slot).wait()

        for slot in range(2):
            j = i * 2 + slot
            start = pl.multiple_of(j * TILE, TILE)
            here = mask_row(start, TILE)
            for r in range(0, hid, CHUNK):
                rows = slice(r, r + CHUNK)
                for half in range(2):
                    lanes = slice(half * 128, half * 128 + 128)
                    z = mid_z[rows, pl.ds(start + half * 128, 128)]
                    u = z * bn2[0, rows, :] + bn2[1, rows, :]
                    m = soft_two(u)
                    v = (u - bn2[3, rows, :] * m) * -LN2
                    soft_s[slot, 0, 0, rows, lanes] = v.astype(LOW)
                    soft_s[slot, 1, 0, rows, lanes] = m.astype(LOW)
            s = dot_nn(wht[...], soft_s[slot, 0, 0]) + bias_col
            score_s[slot] = s * here
            s = jnp.where(class_id < C, s, -1e30)
            e = jnp.exp(s - jnp.max(s, axis=0, keepdims=True))
            p = e / jnp.sum(e, axis=0, keepdims=True)
            trained = here * marked_ref[:, pl.ds(start, TILE)].astype(WIDE)
            hot = (class_id == label_ref[:, pl.ds(start, TILE)]).astype(WIDE)
            g = ((p - hot) * trained).astype(LOW)
            bias_acc[...] += fold_halves(g.astype(WIDE))
            head_acc[...] += dot_nt(g, soft_s[slot, 0, 0])
            pre_s[slot] = dot_nn(whn[:, 0:48], g)
            for r in range(0, hid, CHUNK):
                rows = slice(r, r + CHUNK)
                sums = [0.0, 0.0, 0.0]
                for half in range(2):
                    lanes = slice(half * 128, half * 128 + 128)
                    d = pre_s[slot, rows, lanes]
                    m = soft_s[slot, 1, 0, rows, lanes].astype(WIDE)
                    c3 = bn2[3, rows, :]
                    dy = d * ((1.0 - c3) + c3 * jnp.exp2(-m))
                    z = mid_z[rows, pl.ds(start + half * 128, 128)] - bn2[2, rows, :]
                    sums[0] += d * m
                    sums[1] += dy
                    sums[2] += dy * z
                    dz[rows, pl.ds(start + half * 128, 128)] = dy.astype(LOW)
                for q in range(3):
                    acc[q, rows, :] += sums[q]
        for slot in range(2):
            score_save(slot, 2 * i + slot).start()
        return carry

    lax.fori_loop(0, tiles // 2, head, 0)
    for slot in range(2):
        score_save(slot, tiles - 2 + slot).wait()

    put_rows(1, 0, rows_of(1))
    put_rows(1, blocks, rows_of(2))
    share_start(1, 5)
    share_mid(1, 5)
    flat = jnp.concatenate(
        [head_acc[:, q * FP : (q + 1) * FP] for q in range(blocks)]
        + [
            jnp.concatenate(
                [bias_acc[...], jnp.zeros((FP - 48, FP), WIDE)], axis=0
            ).T.sum(axis=0, keepdims=True).reshape(1, FP),
            jnp.zeros((7, FP), WIDE),
        ],
        axis=0,
    )
    rows_h = head_loc.shape[2]
    slope_row = rows_of(0) * -LN2
    flat = jnp.concatenate(
        [flat]
        + [slope_row[:, q * FP : (q + 1) * FP] for q in range(blocks)]
        + [jnp.zeros((2 * nch * rows_h - 200 - blocks, FP), WIDE)],
        axis=0,
    )
    head_loc[...] = flat.reshape(nch, 2, rows_h, FP)
    to_sibling(6, head_loc.at[:, 1 - core], head_sib).start()
    tot = share_end(1, 5)

    for q in range(blocks):
        here = slice(q * FP, (q + 1) * FP)
        mean, inv, gain = means[q]
        grad_shift = tot[q : q + 1]
        grad_gain = tot[blocks + q : blocks + q + 1] * inv
        a = gain * inv
        slope = a * grad_gain * inv / filled
        bn2[0, here, :] = column(a)
        bn2[1, here, :] = column(slope)
        bn2[2, here, :] = column(a * grad_shift / filled - slope * mean)
        msg_own[0, q : q + 1, :] = grad_gain
        msg_own[0, blocks + q : blocks + q + 1, :] = grad_shift

    def mid_back(j, carry):
        start = pl.multiple_of(j * TILE, TILE)
        here = mask_row(start, TILE)
        for r in range(0, hid, CHUNK):
            rows = slice(r, r + CHUNK)
            for half in range(2):
                at = pl.ds(start + half * 128, 128)
                d = dz[rows, at].astype(WIDE) * bn2[0, rows, :]
                t = mid_z[rows, at] * bn2[1, rows, :] + bn2[2, rows, :]
                dz[rows, at] = (d - t * here[:, half * 128 : half * 128 + 128]).astype(LOW)
        return carry

    lax.fori_loop(0, tiles, mid_back, 0)

    to_sibling(6, head_loc.at[:, 1 - core], head_sib).wait()
    reduce_two(6, head_loc, head_sib, head_in)

    width_m = K * hid

    def mid_grad(i, carry):
        at = pl.ds(pl.multiple_of(i * TILE, TILE), TILE)
        pre_s[0] = dot_nt(dz[...], cat[at, :])
        for c in range(nch):
            first = pre_s[0, 2 * c * rb : (2 * c + 1) * rb, :]
            second = pre_s[0, (2 * c + 1) * rb : (2 * c + 2) * rb, :]
            mid_z[c * rb : (c + 1) * rb, at] = jnp.where(core == 0, first, second)
            wm_all[c, 0, :, at] = jnp.where(core == 0, second, first).astype(LOW)
        return carry

    piece = width_m // K

    def mid_slot(c):
        return 8 if c == 0 else 13 + c

    def mid_pass(c):
        at = pl.ds(c * piece, piece)
        return to_sibling(mid_slot(c), wm_all.at[:, 0, :, at], wm_all.at[:, 1, :, at])

    def mid_send(c, s):
        at = pl.ds(c * piece, piece)
        return to_peer(
            mid_slot(c),
            s,
            wm_all.at[lax.rem(chip + s, nch), 0, :, at],
            gm_in.at[chip, :, at],
        )

    def mid_add(c):
        mid_pass(c).wait()
        at = slice(c * piece, (c + 1) * piece)
        for n in range(nch):
            v = mid_z[n * rb : (n + 1) * rb, at] + wm_all[n, 1, :, at].astype(WIDE)
            wm_all[n, 0, :, at] = v.astype(LOW)
        for s in range(1, nch):
            mid_send(c, s).start()
        gm_in[chip, :, at] = wm_all[chip, 0, :, at]

    steps = piece // TILE
    for c in range(K):
        lax.fori_loop(c * steps, (c + 1) * steps, mid_grad, 0)
        mid_pass(c).start()
        if c > 0:
            mid_add(c - 1)
    reduce_wait(6, head_loc, head_in)
    head_all[chip, core] = total_of(head_in)
    spread_one(7, head_all)

    groups = tiles // GROUP

    def soft_load(t):
        k = lax.div(t, groups)
        g = lax.rem(t, groups)
        slot = lax.rem(t, 2)
        return pltpu.make_async_copy(
            soft_hbm.at[:, pl.ds(g * GROUP, GROUP), k], soft_s.at[slot], soft_sem.at[slot]
        )

    def part_save(k):
        return pltpu.make_async_copy(
            dz.at[pl.ds(k * 112, 112), :], part_hbm.at[k], part_sem.at[k]
        )

    def back_dot(k, j, slot, half):
        rows = slice(half * hid // 2, (half + 1) * hid // 2)
        at = slice(k * hid + half * hid // 2, k * hid + (half + 1) * hid // 2)
        w = jnp.concatenate([cat_s[0, at, :], cat_s[1, at, :]], axis=1)
        pre_s[slot, rows, :] = dot_nn(w, dz[:, pl.ds(pl.multiple_of(j * TILE, TILE), TILE)])

    def turned(k):
        rows = slice(k * FP, (k + 1) * FP)
        return jnp.concatenate([wp[2, rows, :], wp[3, rows, :]], axis=1)

    def sum_dot(k, j, slot):
        x = xa[k, :, pl.ds(pl.multiple_of(j * TILE, TILE), TILE)]
        acc[2] += dot_nt(wp[slot], x)

    def part_dot(k):
        def step(i, carry):
            at = pl.ds(pl.multiple_of(i * 4 * TILE, TILE), 4 * TILE)
            dz[k * 112 : (k + 1) * 112, at] = dot_nn(
                turned(k)[0:112], cat[k * hid : (k + 1) * hid, at]
            ).astype(LOW)
            return carry

        lax.fori_loop(0, tiles // 4, step, 0)
        part_save(k).start()

    for t in range(2):
        soft_load(t).start()
    for k in range(K):
        acc[0] = jnp.zeros(acc.shape[1:], WIDE)
        acc[1] = jnp.zeros(acc.shape[1:], WIDE)
        acc[2] = jnp.zeros(acc.shape[1:], WIDE)
        wp[1] = jnp.zeros(wp.shape[1:], LOW)
        back_dot(k, 0, 0, 0)
        back_dot(k, 0, 0, 1)

        def backward(g, carry):
            t = k * groups + g
            side = lax.rem(t, 2)
            soft_load(t).wait()
            for q in range(GROUP):
                j = g * GROUP + q
                slot = q % 2
                after = jnp.minimum(j + 1, tiles - 1)
                before = jnp.maximum(j - 1, 0)
                parts = [
                    functools.partial(back_dot, k, after, 1 - slot, 0),
                    functools.partial(back_dot, k, after, 1 - slot, 1),
                    functools.partial(sum_dot, k, before, 1 - slot),
                ]
                cuts = [0, 3 * hid // 8, 6 * hid // 8, hid]
                for n, part in enumerate(parts):
                    part()
                    for r in range(*cuts[n : n + 2], CHUNK):
                        rows = slice(r, r + CHUNK)
                        wide_rows = slice(k * hid + r, k * hid + r + CHUNK)
                        sums = [0.0, 0.0]
                        for half in range(2):
                            lanes = slice(half * 128, half * 128 + 128)
                            d = pre_s[slot, rows, lanes]
                            m1 = soft_s[side, 0, q, rows, lanes].astype(WIDE)
                            m2 = soft_s[side, 1, q, rows, lanes].astype(WIDE)
                            c2 = cols[1, wide_rows, :]
                            da = d * ((1.0 - c2) + c2 * jnp.exp2(-m2))
                            v = da * (
                                cols[0, wide_rows, :] + cols[2, wide_rows, :] * jnp.exp2(-m1)
                            )
                            sums[0] += d * m2
                            sums[1] += da * m1
                            v = v.astype(LOW)
                            wp[slot, rows, lanes] = v
                            cat[wide_rows, pl.ds(pl.multiple_of(j * TILE + half * 128, 128), 128)] = v
                        acc[0, rows, :] += sums[0]
                        acc[1, rows, :] += sums[1]

            @pl.when(t + 2 < K * groups)
            def _():
                soft_load(t + 2).start()

            return carry

        lax.fori_loop(0, groups, backward, 0)
        sum_dot(k, tiles - 1, 1)

        two = lax.broadcasted_iota(jnp.int32, (hid, FP), 1)
        sl2 = jnp.sum(acc[0], axis=1, keepdims=True) * -LN2
        sl1 = jnp.sum(acc[1], axis=1, keepdims=True) * -LN2
        p = jnp.where(two == F + 4, sl1, jnp.where(two == F + 5, sl2, acc[2]))
        if k > 1:
            reduce_wait(9 + k - 2, pgrad.at[k % 2], pgrad_in.at[k - 2])
        pgrad[k % 2] = p.reshape(nch, 2, rb, FP)
        to_sibling(9 + k, pgrad.at[k % 2, :, 1 - core], pgrad_sib.at[k]).start()

        if k == 0:
            mid_add(K - 1)
            spread_two(7, head_all)
        if k == 1:
            spread_wait(7, head_all)
        if k > 0:
            to_sibling(9 + k - 1, pgrad.at[(k - 1) % 2, :, 1 - core], pgrad_sib.at[k - 1]).wait()
            reduce_two(9 + k - 1, pgrad.at[(k - 1) % 2], pgrad_sib.at[k - 1], pgrad_in.at[k - 1])

    k = K - 1
    part_dot(0)
    to_sibling(9 + k, pgrad.at[k % 2, :, 1 - core], pgrad_sib.at[k]).wait()
    reduce_two(9 + k, pgrad.at[k % 2], pgrad_sib.at[k], pgrad_in.at[k])
    part_dot(1)
    part_dot(2)
    for c in range(K):
        for s in range(1, nch):
            mid_send(c, s).wait()
    gm_out[...] = total_of(gm_in)
    for k in range(K - 2, K):
        reduce_wait(9 + k, pgrad.at[k % 2], pgrad_in.at[k])

    lane_s = lax.broadcasted_iota(jnp.int32, (rb, FP), 1)
    quant = []
    for k in range(K):
        g = branch_gram(k)
        w = wb_own[k]
        wf, wg, mean, inv, filled = branch_stats(w, g, split_three(g))
        p = total_of(pgrad_in.at[k])
        st = p[:, F : F + 1]
        tz = jnp.sum(jnp.where(lane_s < F, p * wf, 0.0), axis=1, keepdims=True)
        gt = (tz - mean * st) * inv
        totals = g[F : F + 1, :]
        gb_out[k] = p - (st * totals + gt * inv * (wg - mean * totals)) / filled
        q0 = gt * inv / filled
        q1 = st / filled - q0 * mean
        vals = [st, gt, p[:, F + 4 : F + 5], p[:, F + 5 : F + 6], q0, q1, inv]
        block = jnp.zeros((rb, FP), WIDE)
        for n, v in enumerate(vals):
            block = jnp.where(lane_s == n, v, block)
        quant.append(block)
    quant = jnp.concatenate(quant + [jnp.zeros((FP - K * rb, FP), WIDE)], axis=0).T
    rows_own[...] = quant[0:8, :]
    rows_all[chip, core] = rows_own[...]
    spread_one(13, rows_all)
    part_dot(3)
    spread_two(13, rows_all)
    spread_wait(13, rows_all)
    for k in range(K):
        part_save(k).wait()
    full = []
    per = FP // rb
    lane8 = lax.broadcasted_iota(jnp.int32, (8, FP), 1)
    for k in range(K):
        for t in range(hid // FP):
            v = jnp.zeros((8, FP), WIDE)
            for n in range(per):
                d = t * per + n
                piece = rows_all[d // 2, d % 2]
                moved = pltpu.roll(piece, (n * rb - k * rb) % FP, 1)
                v = jnp.where((lane8 >= n * rb) & (lane8 < (n + 1) * rb), moved, v)
            full.append(v)
    for c in range(K * blocks):
        v = full[c]
        gain = small_ref[c : c + 1, :]
        unit = gain * v[6:7]
        rows_out[c : c + 1, :] = v[1:2] / unit
        rows_out[K * blocks + c : K * blocks + c + 1, :] = v[0:1] / unit
        rows_out[2 * K * blocks + c : 2 * K * blocks + c + 1, :] = v[2:3]
        rows_out[3 * K * blocks + c : 3 * K * blocks + c + 1, :] = v[3:4]
    rows_out[base : base + 2 * blocks, :] = msg_own[0, 0 : 2 * blocks, :]
    head_flat = head_all[...].reshape(2 * nch * rows_h, FP)
    rows_out[base + 2 * blocks : base + 3 * blocks, :] = head_flat[200 : 200 + blocks]
    rows_out[base + 3 * blocks : base + 3 * blocks + 1, :] = head_flat[192:193]
    rows_out[base + 3 * blocks + 1 :, :] = jnp.zeros(
        (rows_out.shape[0] - base - 3 * blocks - 1, FP), WIDE
    )
    for q in range(blocks):
        head_out[:, q * FP : (q + 1) * FP] = head_flat[q * 48 : q * 48 + 48]
    for k in range(K):
        wt = turned(k).astype(WIDE)
        r0 = jnp.concatenate([full[k * blocks + q][4:5] for q in range(blocks)], axis=1)
        r1 = jnp.concatenate([full[k * blocks + q][5:6] for q in range(blocks)], axis=1)
        m = dot_nt((wt * r0).astype(LOW), turned(k))
        v = jnp.sum(wt * r1, axis=1, keepdims=True)
        corr_out[k] = jnp.where(lane == F, v, m).astype(LOW)


def finish_kernel(
    root,
    count_ref,
    feats_ref,
    part_ref,
    corr_ref,
    score_ref,
    gm_ref,
    gb_ref,
    gh_ref,
    *refs,
):
    states, outs = refs[:9], refs[9:]
    grad_ref, logit_ref, grad_b, grad_h, grad_m = outs[:5]
    new = outs[5:]
    width = feats_ref.shape[1]
    lane = lax.broadcasted_iota(jnp.int32, (1, width), 1) + pl.program_id(0) * width
    here = (lane < count_ref[0]).astype(WIDE)
    row_id = lax.broadcasted_iota(jnp.int32, (112, width), 0)
    x = feats_ref[...].astype(WIDE)
    x = jnp.concatenate([x, jnp.zeros((16, width), WIDE)], axis=0)
    for k in range(K):
        piece = x[k * F : k * F + 112]
        piece = jnp.where(row_id < F, piece * here, jnp.where(row_id < F + 1, here, 0.0))
        fix = dot_nn(corr_ref[k, 0:112, 0:112], piece.astype(LOW))
        out = part_ref[k].astype(WIDE) - fix
        grad_ref[k * F : (k + 1) * F, :] = out[0:F]
    logit_ref[...] = score_ref[0:C, :]

    @pl.when(pl.program_id(0) == 0)
    def _():
        g = jnp.concatenate([gb_ref[k][:, 0:F] for k in range(K)], axis=1)
        grad_b[...] = g
        grad_h[...] = gh_ref[0:C, :]
        grad_m[...] = gm_ref[...]
        for n, (grad, rate) in enumerate(
            ((g, 0.8 / root), (gm_ref[...], 0.08 / root), (gh_ref[0:C, :], 0.3 / root))
        ):
            w, m, a = (r[...] for r in states[3 * n : 3 * n + 3])
            res = nesterov(w, grad, m, a, rate)
            for r, v in zip(new[3 * n : 3 * n + 3], res):
                r[...] = v


def fused(
    features,
    counts,
    labelled,
    labels,
    w_branch,
    w_mid,
    w_head,
    small_params,
    mom_branch,
    mom_mid,
    mom_head,
    mom_small,
    avg_branch,
    avg_mid,
    avg_head,
    avg_small,
):
    nodes = features.shape[0]
    devices = lax.axis_size("shard")
    nch = devices // 2
    rb = w_mid.shape[1]
    tiles = nodes // TILE
    rows_g = K * FP // devices
    rows_h = 8
    feats = features.T
    small_rows = -(-small_params.shape[0] // (8 * FP)) * 8
    small = jnp.pad(small_params, (0, small_rows * FP - small_params.shape[0])).reshape(
        small_rows, FP
    )
    vmem = pl.BlockSpec(memory_space=pltpu.VMEM)
    hbm = pl.BlockSpec(memory_space=pl.ANY)
    smem = pl.BlockSpec(memory_space=pltpu.SMEM)
    width_m = K * H
    scores, part, soft, gm, gb, gh, gs, corr = pl.pallas_call(
        functools.partial(net_kernel, nch),
        out_shape=(
            jax.ShapeDtypeStruct((48, nodes), WIDE),
            jax.ShapeDtypeStruct((K, 112, nodes), LOW),
            jax.ShapeDtypeStruct((2, tiles, K, H, TILE), LOW),
            jax.ShapeDtypeStruct((rb, width_m), WIDE),
            jax.ShapeDtypeStruct((K, rb, FP), WIDE),
            jax.ShapeDtypeStruct((48, H), WIDE),
            jax.ShapeDtypeStruct((small_rows, FP), WIDE),
            jax.ShapeDtypeStruct((K, FP, FP), LOW),
        ),
        in_specs=[smem, hbm] + [vmem] * 6,
        out_specs=(hbm, hbm, hbm, vmem, vmem, vmem, vmem, vmem),
        scratch_shapes=[
            pltpu.VMEM((K, FP, nodes), LOW),
            pltpu.VMEM((width_m, nodes), LOW),
            pltpu.VMEM((H, nodes), WIDE),
            pltpu.VMEM((H, nodes), LOW),
            pltpu.VMEM((2, width_m, TILE), LOW),
            pltpu.VMEM((2, 2, K, H, TILE), LOW),
            pltpu.VMEM((2, H, TILE), WIDE),
            pltpu.VMEM((K, H, 2 * FP), LOW),
            pltpu.VMEM((3, width_m, FP), WIDE),
            pltpu.VMEM((K, rb, FP), LOW),
            pltpu.VMEM((K, nch, 2, rb, FP), LOW),
            pltpu.VMEM((rb, width_m), LOW),
            pltpu.VMEM((nch, 2, rb, width_m), LOW),
            pltpu.VMEM((nch, 2, rows_g, FP), WIDE),
            pltpu.VMEM((nch, rows_g, FP), WIDE),
            pltpu.VMEM((nch, rows_g, FP), WIDE),
            pltpu.VMEM((nch, 2, rows_g, FP), WIDE),
            pltpu.VMEM((48, H), LOW),
            pltpu.VMEM((H, FP), LOW),
            pltpu.VMEM((FP, FP), WIDE),
            pltpu.VMEM((3, H, FP), WIDE),
            pltpu.VMEM((2, 8, FP), WIDE),
            pltpu.VMEM((2, 8, FP), WIDE),
            pltpu.VMEM((2, nch, 8, FP), WIDE),
            pltpu.VMEM((4, H, FP), WIDE),
            pltpu.VMEM((48, H), WIDE),
            pltpu.VMEM((48, FP), WIDE),
            pltpu.VMEM((nch, 2, rows_h, FP), WIDE),
            pltpu.VMEM((nch, rows_h, FP), WIDE),
            pltpu.VMEM((nch, rows_h, FP), WIDE),
            pltpu.VMEM((nch, 2, rows_h, FP), WIDE),
            pltpu.VMEM((2, nch, 2, rb, FP), WIDE),
            pltpu.VMEM((K, nch, rb, FP), WIDE),
            pltpu.VMEM((K, nch, rb, FP), WIDE),
            pltpu.VMEM((nch, rb, width_m), LOW),
            pltpu.VMEM((8, FP), WIDE),
            pltpu.VMEM((nch, 2, 8, FP), WIDE),
            pltpu.VMEM((2, 48, TILE), WIDE),
            pltpu.SemaphoreType.DMA((1,)),
            pltpu.SemaphoreType.DMA((2,)),
            pltpu.SemaphoreType.DMA((K,)),
            pltpu.SemaphoreType.DMA((2,)),
            pltpu.SemaphoreType.DMA((17, nch)),
            pltpu.SemaphoreType.DMA((17, nch)),
        ],
        compiler_params=pltpu.CompilerParams(
            collective_id=0, has_side_effects=True, vmem_limit_bytes=65400 * 1024
        ),
    )(counts, feats, labels.reshape(1, nodes), labelled.reshape(1, nodes), w_branch.T, w_mid.T, w_head.T, small)
    step = nodes // 2
    root = math.sqrt(nodes * devices)

    def whole(v):
        return pl.BlockSpec(v.shape, lambda i: (0,) * len(v.shape))

    states = (
        w_branch.T,
        mom_branch.T,
        avg_branch.T,
        w_mid.T,
        mom_mid.T,
        avg_mid.T,
        w_head.T,
        mom_head.T,
        avg_head.T,
    )
    shapes = [jax.ShapeDtypeStruct(v.shape, WIDE) for v in (states[0], states[6], gm) + states]
    fgrad, logits, grad_b, grad_h, grad_m, *new = pl.pallas_call(
        functools.partial(finish_kernel, root),
        grid=(nodes // step,),
        out_shape=[
            jax.ShapeDtypeStruct((K * F, nodes), WIDE),
            jax.ShapeDtypeStruct((C, nodes), WIDE),
        ]
        + shapes,
        in_specs=[
            smem,
            pl.BlockSpec((K * F, step), lambda i: (0, i)),
            pl.BlockSpec((K, 112, step), lambda i: (0, 0, i)),
            pl.BlockSpec((K, FP, FP), lambda i: (0, 0, 0)),
            pl.BlockSpec((48, step), lambda i: (0, i)),
        ]
        + [whole(v) for v in (gm, gb, gh) + states],
        out_specs=[
            pl.BlockSpec((K * F, step), lambda i: (0, i)),
            pl.BlockSpec((C, step), lambda i: (0, i)),
        ]
        + [whole(v) for v in shapes],
        compiler_params=pltpu.CompilerParams(vmem_limit_bytes=65400 * 1024),
    )(counts, feats, part, corr, scores, gm, gb, gh, *states)
    grad_small = gs.reshape(-1)[: small_params.shape[0]]
    mom_b, avg_b, new_b, mom_m, avg_m, new_m, mom_h, avg_h, new_h = (v.T for v in new)
    mom_s, avg_s, new_s = nesterov(small_params, grad_small, mom_small, avg_small, 1.0 / root)
    return (
        logits.T,
        fgrad.T,
        grad_b.T,
        grad_m.T,
        grad_h.T,
        grad_small,
        mom_b,
        mom_m,
        mom_h,
        mom_s,
        avg_b,
        avg_m,
        avg_h,
        avg_s,
        new_b,
        new_m,
        new_h,
        new_s,
    )


def solution(mesh):
    in_specs = (
        P("shard", None),
        P("shard"),
        P("shard"),
        P("shard"),
        P(None, "shard"),
        P(None, "shard"),
        P(),
        P(),
        P(None, "shard"),
        P(None, "shard"),
        P(),
        P(),
        P(None, "shard"),
        P(None, "shard"),
        P(),
        P(),
    )
    out_specs = (
        P("shard", None),
        P("shard", None),
        P(None, "shard"),
        P(None, "shard"),
        P(),
        P(),
        P(None, "shard"),
        P(None, "shard"),
        P(),
        P(),
        P(None, "shard"),
        P(None, "shard"),
        P(),
        P(),
        P(None, "shard"),
        P(None, "shard"),
        P(),
        P(),
    )
    run = fused if H % (16 * mesh.size) == 0 else local
    return jax.shard_map(run, mesh=mesh, in_specs=in_specs, out_specs=out_specs, check_vma=False)
```
